512 devices in a mesh: space: 64 (over z, y_hi, x), chaos: 8 (over y_lo, core).
Axes of the slice: x: 4, y: 8 (y_hi: 2, y_lo: 4; y = y_hi * 4 + y_lo), z: 8, core: 2. Of those that a mesh axis runs over, the one named last changes fastest.
Arguments:
- adjoint_field: bfloat16 [56, 32768], P('chaos', 'space'), may hold values from -6 to 6
- stiffness_tiles: bfloat16 [7, 256, 3, 128, 128], P(None, 'space'), may hold values from -0.3125 to 0.3125
- offsets: int32 [256, 3], P('space'), may hold values from -2 to 2, as said below
- galerkin: float32 [7, 56, 56], replicated, as said below
- adjoint_rhs: float32 [56, 32768], P('chaos', 'space'), may hold values from -6 to 6
Outputs:
- residual: float32 [56, 32768], P('chaos', 'space')
The draws below stay inside these ranges and needn't reach their ends.
Inputs may be any that keep to these rules, and one draw needn't show every extreme that they name: offsets[r, 0] is 0 and the 3 entries of each row are distinct. Each galerkin[k] is symmetric.
All inputs are finite; a program needn't handle non-finite values.
Results may differ from the reference program's by a relative error of at most 0.0003.
Values may be sent and summed in bfloat16 or wider, within the bound.
No kernel may reach another device: no remote copies, remote signals or barrier semaphores. Data moves between devices by JAX's collectives and lax.ppermute only.
A program may use at most 64 MiB of HBM per device.

```python
import math
import jax
import jax.numpy as jnp
from jax import lax

CHAOS = 56
TERMS = 7
TILE = 128
NEAR = 3
TILES = 256
DOFS = 32768


def draw_offsets(key, part):
    key = jax.random.fold_in(key, 5)
    scores = jax.random.randint(key, (TILES, 4), 0, 1048576) * 4 + jnp.arange(4, dtype=jnp.int32)
    ranking = jnp.argsort(scores, axis=1)
    candidates = jnp.array([-2, -1, 1, 2], jnp.int32)
    picked = jnp.take(candidates, ranking[:, :NEAR - 1])
    return jnp.concatenate([jnp.zeros((TILES, 1), jnp.int32), picked], axis=1)


def draw_galerkin(key, part):
    key = jax.random.fold_in(key, 11)
    sample = jax.random.normal(key, (TERMS, CHAOS, CHAOS), jnp.float32)
    return (sample + jnp.swapaxes(sample, 1, 2)) * (1.0 / math.sqrt(2.0 * TERMS * CHAOS))


def steps_of(stream_key, shape, shards, low, largest):
    gain, own = 1.0, jax.random.fold_in(stream_key, 6)
    for dim, shards_of in shards:
        draws = jnp.exp(jax.random.uniform(jax.random.fold_in(own, dim), (shards_of,), jnp.float32, low / len(shards), largest / len(shards)))
        gain = gain * jnp.repeat(draws, shape[dim] // shards_of).reshape([-1 if axis == dim else 1 for axis in range(len(shape))])
    return gain


def scatter_about(key, extent, scale, bound, shards=(), kind=jnp.bfloat16):
    result = jax.random.normal(key, extent, jnp.float32) * scale
    if len(shards) > 0:
        result = steps_of(key, extent, shards, -0.22, 0.18) * result
    return jnp.clip(result, min=-bound, max=bound).astype(kind)


def setup_inputs(seed: int = 0) -> dict:
    seeds = jax.random.split(jax.random.key(seed), 6)
    adjoint_field = scatter_about(seeds[0], (CHAOS, DOFS), 1.0, 6.0, ((0, 8), (1, 64)))
    stiffness_tiles = scatter_about(seeds[1], (TERMS, TILES, NEAR, TILE, TILE), (NEAR * TILE) ** -0.5, 0.3125, ((1, 64),))
    offsets = draw_offsets(jax.random.fold_in(seeds[5], 71), 0)
    galerkin = draw_galerkin(jax.random.fold_in(seeds[5], 71), 0)
    adjoint_rhs = scatter_about(seeds[4], (CHAOS, DOFS), 1.0, 6.0, ((0, 8), (1, 64)), jnp.float32)
    return dict(adjoint_field=adjoint_field, stiffness_tiles=stiffness_tiles, offsets=offsets, galerkin=galerkin, adjoint_rhs=adjoint_rhs)


def place_table(offsets, slot_count):
    tile_rows = offsets.shape[0]
    target = jnp.arange(tile_rows, dtype=jnp.int32)[:, None] + offsets + 2
    positions = jnp.arange(slot_count, dtype=jnp.int32)
    return (target[:, :, None] == positions[None, None, :]).astype(jnp.float32)


def reference(adjoint_field, stiffness_tiles, offsets, galerkin, adjoint_rhs):
    blocks = adjoint_field.astype(jnp.float32).reshape(CHAOS, TILES, TILE)
    placing = place_table(offsets, TILES + 4)
    combined = jnp.zeros((CHAOS, TILES, NEAR, TILE), jnp.float32)
    for term_index in range(TERMS):
        contrib = jnp.einsum("prb,rsbc->rspc", blocks, stiffness_tiles[term_index].astype(jnp.float32))
        combined = combined + jnp.einsum("pq,rspc->qrsc", galerkin[term_index], contrib, precision=lax.Precision.HIGHEST)
    extended = jnp.einsum("rst,qrsc->qtc", placing, combined, precision=lax.Precision.HIGHEST)
    applied = extended[:, 2:TILES + 2].reshape(CHAOS, TILES * TILE)
    return adjoint_rhs - applied
```

```python
import jax
import jax.numpy as jnp
from jax import lax
from jax.experimental import pallas as pl
from jax.experimental.pallas import tpu as pltpu
from jax.sharding import PartitionSpec as P

ROWS = 8
REACH = 2


def split(x):
    high = x.astype(jnp.bfloat16)
    low = (x - high.astype(jnp.float32)).astype(jnp.bfloat16)
    return high, low


def tiles_kernel(
    where_ref, offsets_ref, field_ref, tiles_ref, galerkin_ref, rhs_ref,
    main_ref, first_ref, second_ref, gathered, mixer, slots,
):
    terms, tile_rows, near, size, _ = tiles_ref.shape
    groups, own, dofs = field_ref.shape
    chaos = groups * own
    space, far_first = where_ref[0], where_ref[2]
    for g in range(groups):
        gathered[g * own : (g + 1) * own, :] = field_ref[g].astype(jnp.float32)
    field = gathered[...].astype(jnp.bfloat16)
    mixer[...] = jnp.zeros_like(mixer)
    for b in range(2):
        start = where_ref[1 + 2 * b] * own
        for k in range(terms):
            mixer[b, k, :own, :] = galerkin_ref[k, pl.ds(start, own), :]
    mix_high, mix_low = split(mixer[...].reshape(2 * terms * ROWS, chaos))
    mixed = jnp.dot(mix_high, field, preferred_element_type=jnp.float32)
    mixed += jnp.dot(mix_low, field, preferred_element_type=jnp.float32)
    mixed = mixed.reshape(2, terms, ROWS, dofs)
    high = mixed.astype(jnp.bfloat16).astype(jnp.float32)
    parts = jnp.concatenate([high[0:1], mixed[0:1] - high[0:1], high[1:2], mixed[1:2] - high[1:2]], axis=0)
    slots[...] = jnp.zeros_like(slots)
    for r in range(tile_rows):
        left = jnp.concatenate(
            [parts[:, k, :, r * size : (r + 1) * size].reshape(4 * ROWS, size) for k in range(terms)],
            axis=1,
        ).astype(jnp.bfloat16)
        right = jnp.concatenate(
            [tiles_ref[:, r, s].reshape(terms * size, size) for s in range(near)], axis=1
        )
        product = jnp.dot(left, right, preferred_element_type=jnp.float32)
        product = product.reshape(2, 2, ROWS, near * size)
        product = (product[:, 0] + product[:, 1]).reshape(2 * ROWS, near * size)
        for s in range(near):
            slot = r + REACH + offsets_ref[r, s]
            slots[slot] += product[:, s * size : (s + 1) * size]
    for t in range(tile_rows):
        main_ref[:, t * size : (t + 1) * size] = (
            rhs_ref[:, t * size : (t + 1) * size] - slots[t + REACH, :own]
        )
    even = lax.rem(space, 2) == 0
    for t in range(REACH):
        low_a, low_b = slots[t, :ROWS], slots[t, ROWS:]
        top_a, top_b = slots[tile_rows + REACH + t, :ROWS], slots[tile_rows + REACH + t, ROWS:]
        columns = slice(t * size, (t + 1) * size)
        far = jnp.where(even, low_b, top_b)
        near_by = jnp.where(even, low_a, top_a)
        first_ref[:, columns] = jnp.where(far_first == 1, far, near_by)
        second_ref[:, columns] = jnp.where(even, top_a, low_a)


def body(adjoint_field, stiffness_tiles, offsets, galerkin, adjoint_rhs):
    terms, tile_rows, near, size, _ = stiffness_tiles.shape
    own, dofs = adjoint_field.shape
    groups, slabs = lax.axis_size("chaos"), lax.axis_size("space")
    chaos = own * groups
    row = 4
    turn = groups // 2
    space, block = lax.axis_index("space"), lax.axis_index("chaos")
    at_end = ((space % row) == 0) | ((space % row) == row - 1)
    other = jnp.bitwise_xor(block, turn)
    where = jnp.stack([space, block, at_end.astype(jnp.int32), other]).astype(jnp.int32)

    copies = jnp.broadcast_to(adjoint_field[None], (groups, own, dofs))
    field = lax.all_to_all(copies, "chaos", 0, 0)

    halo = REACH * size
    smem = pl.BlockSpec(memory_space=pltpu.SMEM)
    vmem = pl.BlockSpec(memory_space=pltpu.VMEM)
    main, first, second = pl.pallas_call(
        tiles_kernel,
        out_shape=(
            jax.ShapeDtypeStruct((own, dofs), jnp.float32),
            jax.ShapeDtypeStruct((ROWS, halo), jnp.float32),
            jax.ShapeDtypeStruct((ROWS, halo), jnp.float32),
        ),
        in_specs=[smem, smem, vmem, vmem, vmem, vmem],
        out_specs=(vmem, vmem, vmem),
        scratch_shapes=[
            pltpu.VMEM((chaos, dofs), jnp.float32),
            pltpu.VMEM((2, terms, ROWS, chaos), jnp.float32),
            pltpu.VMEM((tile_rows + 2 * REACH, 2 * ROWS, size), jnp.float32),
        ],
        compiler_params=pltpu.CompilerParams(vmem_limit_bytes=32 * 1024 * 1024),
    )(where, offsets, field, stiffness_tiles, galerkin, adjoint_rhs)

    def swaps(parity):
        pairs = []
        for s in range(parity, slabs - 1, 2):
            for c in range(groups):
                d = c ^ turn if s % row == row - 1 else c
                pairs += [(s * groups + c, (s + 1) * groups + d), ((s + 1) * groups + d, s * groups + c)]
        return pairs

    got_first = lax.ppermute(first, ("space", "chaos"), swaps(1))
    got_second = lax.ppermute(second, ("space", "chaos"), swaps(0))
    even = (space % 2) == 0
    got = jnp.where(
        even,
        jnp.concatenate([got_first, got_second], axis=1),
        jnp.concatenate([got_second, got_first], axis=1),
    )
    return main - got[:own]


def solution(mesh):
    return jax.shard_map(
        body,
        mesh=mesh,
        in_specs=(
            P("chaos", "space"),
            P(None, "space", None, None, None),
            P("space", None),
            P(),
            P("chaos", "space"),
        ),
        out_specs=P("chaos", "space"),
        check_vma=False,
    )
```

```python
import jax
import jax.numpy as jnp
from jax import lax
from jax.experimental import pallas as pl
from jax.experimental.pallas import tpu as pltpu
from jax.sharding import PartitionSpec as P

ROWS = 8
REACH = 2
SPAN = 2 * REACH + 1
RUN = 4


def split(x):
    high = x.astype(jnp.bfloat16)
    low = (x - high.astype(jnp.float32)).astype(jnp.bfloat16)
    return high, low


def in_hbm(x):
    return pltpu.with_memory_space_constraint(x, pltpu.HBM)


def stage_kernel(
    offsets_ref, tiles_ref, galerkin_ref, rhs_ref,
    tiles_out, mixer_out, masks_out, rhs_out, galerkin, mixer, sems,
):
    terms, tile_rows, near, _, _ = tiles_ref.shape
    own = rhs_ref.shape[0]
    groups = galerkin_ref.shape[1] // own
    moves = [
        pltpu.make_async_copy(galerkin_ref, galerkin, sems.at[0]),
        pltpu.make_async_copy(rhs_ref, rhs_out, sems.at[1]),
    ]
    for k in range(terms):
        moves.append(pltpu.make_async_copy(tiles_ref.at[k], tiles_out.at[k], sems.at[2 + k]))
    for move in moves:
        move.start()
    space, block = lax.axis_index("space"), lax.axis_index("chaos")
    def row_of(flag):
        return jnp.full((1, masks_out.shape[1]), flag.astype(jnp.float32))
    for r in range(tile_rows):
        for s in range(near):
            for o in range(SPAN):
                at = (r * near + s) * SPAN + o
                masks_out[at : at + 1, :] = row_of(offsets_ref[r, s] == o - REACH)
    at = tile_rows * near * SPAN
    place = lax.rem(space, RUN)
    masks_out[at : at + 1, :] = row_of(lax.rem(space, 2) == 0)
    masks_out[at + 1 : at + 2, :] = row_of(jnp.logical_or(place == 0, place == RUN - 1))
    mixer[...] = jnp.zeros_like(mixer)
    moves[0].wait()
    half = groups // 2
    other = jnp.where(block < half, block + half, block - half)
    for b, owner in enumerate((block, other)):
        for k in range(terms):
            mixer[b, k, :own, :] = galerkin[k, pl.ds(owner * own, own), :]
    high, low = split(mixer[...].reshape(2 * terms * ROWS, groups * own))
    mixer_out[0], mixer_out[1] = high, low
    for move in moves[1:]:
        move.wait()


def tiles_kernel(
    field_ref, tiles_ref, mixer_ref, masks_ref, rhs_ref,
    main_ref, first_ref, second_ref, gathered,
):
    terms, tile_rows, near, size, _ = tiles_ref.shape
    groups, own, dofs = field_ref.shape
    for g in range(groups):
        gathered[g * own : (g + 1) * own, :] = field_ref[g].astype(jnp.float32)
    field = gathered[...].astype(jnp.bfloat16)
    mixed = jnp.dot(mixer_ref[0], field, preferred_element_type=jnp.float32)
    mixed += jnp.dot(mixer_ref[1], field, preferred_element_type=jnp.float32)
    mixed = mixed.reshape(2, terms, ROWS, dofs)
    high = mixed.astype(jnp.bfloat16).astype(jnp.float32)
    low = mixed - high
    slots = [jnp.zeros((2 * ROWS, size), jnp.float32) for _ in range(tile_rows + 2 * REACH)]
    for r in range(tile_rows):
        columns = slice(r * size, (r + 1) * size)
        left = jnp.concatenate(
            [
                jnp.concatenate([part[b, k, :, columns] for b in range(2) for part in (high, low)], axis=0)
                for k in range(terms)
            ],
            axis=1,
        ).astype(jnp.bfloat16)
        right = jnp.concatenate(
            [tiles_ref[:, r, s].reshape(terms * size, size) for s in range(near)], axis=1
        )
        product = jnp.dot(left, right, preferred_element_type=jnp.float32)
        product = product.reshape(2, 2, ROWS, near * size)
        product = (product[:, 0] + product[:, 1]).reshape(2 * ROWS, near * size)
        slots[r + REACH] += product[:, :size]
        for s in range(1, near):
            entry = product[:, s * size : (s + 1) * size]
            for o in range(SPAN):
                if o == REACH:
                    continue
                at = (r * near + s) * SPAN + o
                slots[r + o] += jnp.where(masks_ref[at : at + 1, :] > 0, entry, 0.0)
    for t in range(tile_rows):
        columns = slice(t * size, (t + 1) * size)
        main_ref[:, columns] = rhs_ref[:, columns] - slots[t + REACH][:own]
    at = tile_rows * near * SPAN
    even = masks_ref[at : at + 1, :] > 0
    far = masks_ref[at + 1 : at + 2, :] > 0
    for t in range(REACH):
        bottom, top = slots[t], slots[tile_rows + REACH + t]
        columns = slice(t * size, (t + 1) * size)
        across = jnp.where(even, bottom, top)
        first_ref[:, columns] = jnp.where(far, across[ROWS:], across[:ROWS])
        second_ref[:, columns] = jnp.where(even, top[:ROWS], bottom[:ROWS])


def body(adjoint_field, stiffness_tiles, offsets, galerkin, adjoint_rhs):
    terms, tile_rows, near, size, _ = stiffness_tiles.shape
    own, dofs = adjoint_field.shape
    groups, slabs = lax.axis_size("chaos"), lax.axis_size("space")
    chaos = own * groups
    turn = groups // 2
    smem = pl.BlockSpec(memory_space=pltpu.SMEM)
    vmem = pl.BlockSpec(memory_space=pltpu.VMEM)
    hbm = pl.BlockSpec(memory_space=pltpu.HBM)
    limit = 24 * 1024 * 1024

    copies = jnp.broadcast_to(adjoint_field[None], (groups, own, dofs))
    field = lax.all_to_all(copies, "chaos", 0, 0)

    n_masks = tile_rows * near * SPAN + 2
    n_masks += -n_masks % 8
    tiles, mixer, masks, rhs = pl.pallas_call(
        stage_kernel,
        out_shape=(
            jax.ShapeDtypeStruct(stiffness_tiles.shape, jnp.bfloat16),
            jax.ShapeDtypeStruct((2, 2 * terms * ROWS, chaos), jnp.bfloat16),
            jax.ShapeDtypeStruct((n_masks, size), jnp.float32),
            jax.ShapeDtypeStruct((own, dofs), jnp.float32),
        ),
        in_specs=[smem, hbm, hbm, hbm],
        out_specs=(vmem, vmem, vmem, vmem),
        scratch_shapes=[
            pltpu.VMEM((terms, chaos, chaos), jnp.float32),
            pltpu.VMEM((2, terms, ROWS, chaos), jnp.float32),
            pltpu.SemaphoreType.DMA((2 + terms,)),
        ],
        compiler_params=pltpu.CompilerParams(vmem_limit_bytes=limit),
        cost_estimate=pl.CostEstimate(flops=0, bytes_accessed=6 * 2**20, transcendentals=0),
    )(offsets, in_hbm(stiffness_tiles), in_hbm(galerkin), in_hbm(adjoint_rhs))

    halo = REACH * size
    main, first, second = pl.pallas_call(
        tiles_kernel,
        out_shape=(
            jax.ShapeDtypeStruct((own, dofs), jnp.float32),
            jax.ShapeDtypeStruct((ROWS, halo), jnp.float32),
            jax.ShapeDtypeStruct((ROWS, halo), jnp.float32),
        ),
        in_specs=[vmem] * 5,
        out_specs=(vmem, vmem, vmem),
        scratch_shapes=[pltpu.VMEM((chaos, dofs), jnp.float32)],
        compiler_params=pltpu.CompilerParams(vmem_limit_bytes=limit),
    )(field, tiles, mixer, masks, rhs)

    def partner(s, c):
        return (s + 1) * groups + (c ^ turn if s % RUN == RUN - 1 else c)

    pairs = [(s * groups + c, partner(s, c), s) for s in range(slabs - 1) for c in range(groups)]
    axes = ("space", "chaos")
    out = [(b, a) if s % RUN == 0 else (a, b) for a, b, s in pairs if s % 2 == 0]
    both = [pair for a, b, s in pairs if s % 2 == 1 for pair in ((a, b), (b, a))]
    back = [(b, a) for a, b in out]
    swap = out + back
    got_first = lax.ppermute(first, axes, both)
    got_second = lax.ppermute(second, axes, swap)
    even = (lax.axis_index("space") % 2) == 0
    halo_a = jnp.where(even, got_first, got_second)
    halo_b = jnp.where(even, got_second, got_first)
    got = jnp.concatenate([halo_a, halo_b], axis=1)
    return main - got[:own]


def solution(mesh):
    return jax.shard_map(
        body,
        mesh=mesh,
        in_specs=(
            P("chaos", "space"),
            P(None, "space", None, None, None),
            P("space", None),
            P(),
            P("chaos", "space"),
        ),
        out_specs=P("chaos", "space"),
        check_vma=False,
    )
```

```python
import jax
import jax.numpy as jnp
from jax import lax
from jax.experimental import pallas as pl
from jax.experimental.pallas import tpu as pltpu
from jax.sharding import PartitionSpec as P

ROWS = 8
REACH = 2
SPAN = 2 * REACH + 1
RUN = 4


def in_hbm(x):
    return pltpu.with_memory_space_constraint(x, pltpu.HBM)


def split(x):
    high = x.astype(jnp.bfloat16)
    low = (x - high.astype(jnp.float32)).astype(jnp.bfloat16)
    return high, low


def stage_kernel(
    field_ref, offsets_ref, tiles_ref, galerkin_ref,
    copies_out, tiles_out, mixer_out, masks_out,
    field, offsets, galerkin, mixer, sems,
):
    terms, tile_rows, near, _, _ = tiles_ref.shape
    groups, own, _ = copies_out.shape
    pairs = [(field_ref, field), (galerkin_ref, galerkin), (offsets_ref, offsets)]
    pairs.append((tiles_ref.at[:, :, 1:near], tiles_out))
    moves = [pltpu.make_async_copy(a, b, sems.at[i]) for i, (a, b) in enumerate(pairs)]
    for move in moves:
        move.start()
    space, block = lax.axis_index("space"), lax.axis_index("chaos")
    moves[0].wait()
    value = field[...]
    for g in range(groups):
        copies_out[g] = value
    mixer[...] = jnp.zeros_like(mixer)
    moves[1].wait()
    half = groups // 2
    other = jnp.where(block < half, block + half, block - half)
    for b, owner in enumerate((block, other)):
        for k in range(terms):
            mixer[b, k, :own, :] = galerkin[k, pl.ds(owner * own, own), :]
    high, low = split(mixer[...].reshape(2 * terms * ROWS, groups * own))
    mixer_out[0], mixer_out[1] = high, low
    moves[2].wait()

    def row_of(flag):
        return jnp.full((1, masks_out.shape[1]), flag.astype(jnp.float32))

    for r in range(tile_rows):
        for s in range(1, near):
            for o in range(SPAN):
                at = (r * near + s) * SPAN + o
                masks_out[at : at + 1, :] = row_of(offsets[r, s] == o - REACH)
    at = tile_rows * near * SPAN
    place = lax.rem(space, RUN)
    masks_out[at : at + 1, :] = row_of(lax.rem(space, 2) == 0)
    masks_out[at + 1 : at + 2, :] = row_of(jnp.logical_or(place == 0, place == RUN - 1))
    moves[3].wait()


def mix(field_ref, mixer_ref, gathered, blocks):
    groups, own, dofs = field_ref.shape
    rows = mixer_ref.shape[1] // 2 * blocks
    for g in range(groups):
        gathered[g * own : (g + 1) * own, :] = field_ref[g].astype(jnp.float32)
    field = gathered[...].astype(jnp.bfloat16)
    mixed = jnp.dot(mixer_ref[0, :rows], field, preferred_element_type=jnp.float32)
    mixed += jnp.dot(mixer_ref[1, :rows], field, preferred_element_type=jnp.float32)
    mixed = mixed.reshape(blocks, rows // blocks // ROWS, ROWS, dofs)
    high = mixed.astype(jnp.bfloat16).astype(jnp.float32)
    return high, mixed - high


def times_tiles(parts, columns, right):
    blocks, terms = parts[0].shape[:2]
    left = jnp.concatenate(
        [
            jnp.concatenate([part[b, k, :, columns] for b in range(blocks) for part in parts], axis=0)
            for k in range(terms)
        ],
        axis=1,
    ).astype(jnp.bfloat16)
    product = jnp.dot(left, right, preferred_element_type=jnp.float32)
    product = product.reshape(blocks, 2, ROWS, right.shape[1])
    return (product[:, 0] + product[:, 1]).reshape(blocks * ROWS, right.shape[1])


def halo_kernel(
    field_ref, tiles_ref, mixer_ref, masks_ref,
    first_ref, second_ref, inner_ref, gathered,
):
    terms, tile_rows, others, size, _ = tiles_ref.shape
    parts = mix(field_ref, mixer_ref, gathered, 2)
    slots = [jnp.zeros((2 * ROWS, size), jnp.float32) for _ in range(tile_rows + 2 * REACH)]
    for r in range(tile_rows):
        right = jnp.concatenate(
            [tiles_ref[:, r, s].reshape(terms * size, size) for s in range(others)], axis=1
        )
        product = times_tiles(parts, slice(r * size, (r + 1) * size), right)
        for s in range(others):
            entry = product[:, s * size : (s + 1) * size]
            for o in range(SPAN):
                if o == REACH:
                    continue
                at = (r * (others + 1) + s + 1) * SPAN + o
                slots[r + o] += jnp.where(masks_ref[at : at + 1, :] > 0, entry, 0.0)
    at = tile_rows * (others + 1) * SPAN
    even = masks_ref[at : at + 1, :] > 0
    far = masks_ref[at + 1 : at + 2, :] > 0
    for t in range(REACH):
        bottom, top = slots[t], slots[tile_rows + REACH + t]
        columns = slice(t * size, (t + 1) * size)
        across = jnp.where(even, bottom, top)
        first_ref[:, columns] = jnp.where(far, across[ROWS:], across[:ROWS])
        second_ref[:, columns] = jnp.where(even, top[:ROWS], bottom[:ROWS])
    for t in range(tile_rows):
        inner_ref[:, t * size : (t + 1) * size] = slots[t + REACH][:ROWS]


def inner_kernel(
    field_ref, tiles_ref, mixer_ref, inner_ref, rhs_ref,
    main_ref, tiles, rhs, gathered, sems,
):
    terms, tile_rows, _, size, _ = tiles_ref.shape
    own = field_ref.shape[1]
    get_tiles = pltpu.make_async_copy(tiles_ref.at[:, :, 0], tiles, sems.at[0])
    get_rhs = pltpu.make_async_copy(rhs_ref, rhs, sems.at[1])
    get_tiles.start()
    get_rhs.start()
    parts = mix(field_ref, mixer_ref, gathered, 1)
    get_tiles.wait()
    get_rhs.wait()
    for r in range(tile_rows):
        columns = slice(r * size, (r + 1) * size)
        product = times_tiles(parts, columns, tiles[:, r].reshape(terms * size, size))
        main_ref[:, columns] = rhs[:, columns] - (inner_ref[:, columns] + product)[:own]


def body(adjoint_field, stiffness_tiles, offsets, galerkin, adjoint_rhs):
    terms, tile_rows, near, size, _ = stiffness_tiles.shape
    own, dofs = adjoint_field.shape
    groups, slabs = lax.axis_size("chaos"), lax.axis_size("space")
    chaos = own * groups
    turn = groups // 2
    vmem = pl.BlockSpec(memory_space=pltpu.VMEM)
    hbm = pl.BlockSpec(memory_space=pltpu.HBM)
    params = pltpu.CompilerParams(vmem_limit_bytes=24 * 1024 * 1024)
    all_tiles, rhs = in_hbm(stiffness_tiles), in_hbm(adjoint_rhs)

    n_masks = tile_rows * near * SPAN + 2
    n_masks += -n_masks % 8
    copies, tiles, mixer, masks = pl.pallas_call(
        stage_kernel,
        out_shape=(
            jax.ShapeDtypeStruct((groups, own, dofs), jnp.bfloat16),
            jax.ShapeDtypeStruct((terms, tile_rows, near - 1, size, size), jnp.bfloat16),
            jax.ShapeDtypeStruct((2, 2 * terms * ROWS, chaos), jnp.bfloat16),
            jax.ShapeDtypeStruct((n_masks, size), jnp.float32),
        ),
        in_specs=[hbm] * 4,
        out_specs=(vmem,) * 4,
        scratch_shapes=[
            pltpu.VMEM((own, dofs), jnp.bfloat16),
            pltpu.SMEM(offsets.shape, jnp.int32),
            pltpu.VMEM((terms, chaos, chaos), jnp.float32),
            pltpu.VMEM((2, terms, ROWS, chaos), jnp.float32),
            pltpu.SemaphoreType.DMA((4,)),
        ],
        compiler_params=params,
    )(in_hbm(adjoint_field), in_hbm(offsets), all_tiles, in_hbm(galerkin))

    field = lax.all_to_all(copies, "chaos", 0, 0)

    halo = REACH * size
    first, second, inner = pl.pallas_call(
        halo_kernel,
        out_shape=(
            jax.ShapeDtypeStruct((ROWS, halo), jnp.float32),
            jax.ShapeDtypeStruct((ROWS, halo), jnp.float32),
            jax.ShapeDtypeStruct((ROWS, dofs), jnp.float32),
        ),
        in_specs=[vmem] * 4,
        out_specs=(vmem,) * 3,
        scratch_shapes=[pltpu.VMEM((chaos, dofs), jnp.float32)],
        compiler_params=params,
    )(field, tiles, mixer, masks)

    main = pl.pallas_call(
        inner_kernel,
        out_shape=jax.ShapeDtypeStruct((own, dofs), jnp.float32),
        in_specs=[vmem, hbm, vmem, vmem, hbm],
        out_specs=vmem,
        scratch_shapes=[
            pltpu.VMEM((terms, tile_rows, size, size), jnp.bfloat16),
            pltpu.VMEM((own, dofs), jnp.float32),
            pltpu.VMEM((chaos, dofs), jnp.float32),
            pltpu.SemaphoreType.DMA((2,)),
        ],
        compiler_params=params,
    )(field, all_tiles, mixer, inner, rhs)

    def partner(s, c):
        return (s + 1) * groups + (c ^ turn if s % RUN == RUN - 1 else c)

    pairs = [(s * groups + c, partner(s, c), s) for s in range(slabs - 1) for c in range(groups)]
    axes = ("space", "chaos")

    def swap(x, parity):
        return lax.ppermute(x, axes, [p for a, b, s in pairs if s % 2 == parity for p in ((a, b), (b, a))])

    got_first, got_second = swap(first, 1), swap(second, 0)
    even = (lax.axis_index("space") % 2) == 0
    halo_a = jnp.where(even, got_first, got_second)
    halo_b = jnp.where(even, got_second, got_first)
    got = jnp.concatenate([halo_a, halo_b], axis=1)
    return main - got[:own]


def solution(mesh):
    return jax.shard_map(
        body,
        mesh=mesh,
        in_specs=(
            P("chaos", "space"),
            P(None, "space", None, None, None),
            P("space", None),
            P(),
            P("chaos", "space"),
        ),
        out_specs=P("chaos", "space"),
        check_vma=False,
    )
```

```python
import jax
import jax.numpy as jnp
from jax import lax
from jax.experimental import pallas as pl
from jax.experimental.pallas import tpu as pltpu
from jax.sharding import PartitionSpec as P

ROWS = 8
REACH = 2
SPAN = 2 * REACH + 1
RUN = 4
BLOCKS = 3


def in_hbm(x):
    return pltpu.with_memory_space_constraint(x, pltpu.HBM)


def split(x):
    high = x.astype(jnp.bfloat16)
    low = (x - high.astype(jnp.float32)).astype(jnp.bfloat16)
    return high, low


def stage_kernel(
    field_ref, offsets_ref, tiles_ref, galerkin_ref,
    copies_out, tiles_out, mixer_out, masks_out,
    field, offsets, galerkin, mixer, sems,
):
    terms, tile_rows, near, _, _ = tiles_ref.shape
    groups, own, _ = copies_out.shape
    pairs = [(field_ref, field), (galerkin_ref, galerkin), (offsets_ref, offsets)]
    pairs.append((tiles_ref.at[:, :, 1:near], tiles_out))
    moves = [pltpu.make_async_copy(a, b, sems.at[i]) for i, (a, b) in enumerate(pairs)]
    for move in moves:
        move.start()
    space, block = lax.axis_index("space"), lax.axis_index("chaos")
    moves[0].wait()
    value = field[...]
    for g in range(groups):
        copies_out[g] = value
    mixer[...] = jnp.zeros_like(mixer)
    moves[1].wait()
    half = groups // 2
    near_by = block + 1 - 2 * lax.rem(block, 2)
    far_off = jnp.where(near_by < half, near_by + half, near_by - half)
    for b, owner in enumerate((near_by, far_off, block)):
        for k in range(terms):
            mixer[b, k, :own, :] = galerkin[k, pl.ds(owner * own, own), :]
    high, low = split(mixer[...].reshape(BLOCKS * terms * ROWS, groups * own))
    mixer_out[0], mixer_out[1] = high, low
    moves[2].wait()

    def row_of(flag):
        return jnp.full((1, masks_out.shape[1]), flag.astype(jnp.float32))

    for r in range(tile_rows):
        for s in range(1, near):
            for o in range(SPAN):
                at = (r * near + s) * SPAN + o
                masks_out[at : at + 1, :] = row_of(offsets[r, s] == o - REACH)
    at = tile_rows * near * SPAN
    place = lax.rem(space, RUN)
    masks_out[at : at + 1, :] = row_of(lax.rem(space, 2) == 0)
    masks_out[at + 1 : at + 2, :] = row_of(jnp.logical_or(place == 0, place == RUN - 1))
    moves[3].wait()


def mix(field_ref, mixer_ref, gathered, first, blocks):
    groups, own, dofs = field_ref.shape
    rows = mixer_ref.shape[1] // BLOCKS
    for g in range(groups):
        gathered[g * own : (g + 1) * own, :] = field_ref[g].astype(jnp.float32)
    field = gathered[...].astype(jnp.bfloat16)
    used = slice(first * rows, (first + blocks) * rows)
    mixed = jnp.dot(mixer_ref[0, used], field, preferred_element_type=jnp.float32)
    mixed += jnp.dot(mixer_ref[1, used], field, preferred_element_type=jnp.float32)
    mixed = mixed.reshape(blocks, rows // ROWS, ROWS, dofs)
    high = mixed.astype(jnp.bfloat16).astype(jnp.float32)
    return high, mixed - high


def beside(tiles_ref, r):
    terms, _, others, size, _ = tiles_ref.shape
    return jnp.concatenate(
        [tiles_ref[:, r, s].reshape(terms * size, size) for s in range(others)], axis=1
    )


def add_entries(slots, product, masks_ref, r, others, wanted):
    size = masks_ref.shape[1]
    for s in range(others):
        entry = product[:, s * size : (s + 1) * size]
        for o in range(SPAN):
            if o == REACH or r + o not in wanted:
                continue
            at = (r * (others + 1) + s + 1) * SPAN + o
            slots[r + o] += jnp.where(masks_ref[at : at + 1, :] > 0, entry, 0.0)


def times_tiles(parts, columns, right):
    blocks, terms = parts[0].shape[:2]
    left = jnp.concatenate(
        [
            jnp.concatenate([part[b, k, :, columns] for b in range(blocks) for part in parts], axis=0)
            for k in range(terms)
        ],
        axis=1,
    ).astype(jnp.bfloat16)
    product = jnp.dot(left, right, preferred_element_type=jnp.float32)
    product = product.reshape(blocks, 2, ROWS, right.shape[1])
    return (product[:, 0] + product[:, 1]).reshape(blocks * ROWS, right.shape[1])


def halo_kernel(
    field_ref, tiles_ref, mixer_ref, masks_ref,
    first_ref, second_ref, gathered,
):
    _, tile_rows, others, size, _ = tiles_ref.shape
    parts = mix(field_ref, mixer_ref, gathered, 0, 2)
    wanted = [*range(REACH), *range(tile_rows + REACH, tile_rows + 2 * REACH)]
    slots = {t: jnp.zeros((2 * ROWS, size), jnp.float32) for t in wanted}
    for r in range(tile_rows):
        product = times_tiles(parts, slice(r * size, (r + 1) * size), beside(tiles_ref, r))
        add_entries(slots, product, masks_ref, r, others, wanted)
    at = tile_rows * (others + 1) * SPAN
    even = masks_ref[at : at + 1, :] > 0
    far = masks_ref[at + 1 : at + 2, :] > 0
    for t in range(REACH):
        bottom, top = slots[t], slots[tile_rows + REACH + t]
        columns = slice(t * size, (t + 1) * size)
        across = jnp.where(even, bottom, top)
        first_ref[:, columns] = jnp.where(far, across[ROWS:], across[:ROWS])
        second_ref[:, columns] = jnp.where(even, top[:ROWS], bottom[:ROWS])


def inner_kernel(
    field_ref, all_tiles_ref, tiles_ref, mixer_ref, masks_ref, rhs_ref,
    main_ref, tiles, rhs, gathered, sems,
):
    terms, tile_rows, others, size, _ = tiles_ref.shape
    own = field_ref.shape[1]
    get_tiles = pltpu.make_async_copy(all_tiles_ref.at[:, :, 0], tiles, sems.at[0])
    get_rhs = pltpu.make_async_copy(rhs_ref, rhs, sems.at[1])
    get_tiles.start()
    get_rhs.start()
    parts = mix(field_ref, mixer_ref, gathered, 2, 1)
    wanted = range(REACH, tile_rows + REACH)
    slots = {t: jnp.zeros((ROWS, size), jnp.float32) for t in wanted}
    for r in range(tile_rows):
        product = times_tiles(parts, slice(r * size, (r + 1) * size), beside(tiles_ref, r))
        add_entries(slots, product, masks_ref, r, others, wanted)
    get_tiles.wait()
    get_rhs.wait()
    for r in range(tile_rows):
        columns = slice(r * size, (r + 1) * size)
        product = times_tiles(parts, columns, tiles[:, r].reshape(terms * size, size))
        main_ref[:, columns] = rhs[:, columns] - (slots[r + REACH] + product)[:own]


def body(adjoint_field, stiffness_tiles, offsets, galerkin, adjoint_rhs):
    terms, tile_rows, near, size, _ = stiffness_tiles.shape
    own, dofs = adjoint_field.shape
    groups, slabs = lax.axis_size("chaos"), lax.axis_size("space")
    chaos = own * groups
    turn = groups // 2
    vmem = pl.BlockSpec(memory_space=pltpu.VMEM)
    hbm = pl.BlockSpec(memory_space=pltpu.HBM)
    params = pltpu.CompilerParams(vmem_limit_bytes=24 * 1024 * 1024)
    all_tiles, rhs = in_hbm(stiffness_tiles), in_hbm(adjoint_rhs)

    n_masks = tile_rows * near * SPAN + 2
    n_masks += -n_masks % 8
    copies, tiles, mixer, masks = pl.pallas_call(
        stage_kernel,
        out_shape=(
            jax.ShapeDtypeStruct((groups, own, dofs), jnp.bfloat16),
            jax.ShapeDtypeStruct((terms, tile_rows, near - 1, size, size), jnp.bfloat16),
            jax.ShapeDtypeStruct((2, BLOCKS * terms * ROWS, chaos), jnp.bfloat16),
            jax.ShapeDtypeStruct((n_masks, size), jnp.float32),
        ),
        in_specs=[hbm] * 4,
        out_specs=(vmem,) * 4,
        scratch_shapes=[
            pltpu.VMEM((own, dofs), jnp.bfloat16),
            pltpu.SMEM(offsets.shape, jnp.int32),
            pltpu.VMEM((terms, chaos, chaos), jnp.float32),
            pltpu.VMEM((BLOCKS, terms, ROWS, chaos), jnp.float32),
            pltpu.SemaphoreType.DMA((4,)),
        ],
        compiler_params=params,
    )(in_hbm(adjoint_field), in_hbm(offsets), all_tiles, in_hbm(galerkin))

    field = lax.all_to_all(copies, "chaos", 0, 0)

    halo = REACH * size
    first, second = pl.pallas_call(
        halo_kernel,
        out_shape=(
            jax.ShapeDtypeStruct((ROWS, halo), jnp.float32),
            jax.ShapeDtypeStruct((ROWS, halo), jnp.float32),
        ),
        in_specs=[vmem] * 4,
        out_specs=(vmem,) * 2,
        scratch_shapes=[pltpu.VMEM((chaos, dofs), jnp.float32)],
        compiler_params=params,
    )(field, tiles, mixer, masks)

    main = pl.pallas_call(
        inner_kernel,
        out_shape=jax.ShapeDtypeStruct((own, dofs), jnp.float32),
        in_specs=[vmem, hbm, vmem, vmem, vmem, hbm],
        out_specs=vmem,
        scratch_shapes=[
            pltpu.VMEM((terms, tile_rows, size, size), jnp.bfloat16),
            pltpu.VMEM((own, dofs), jnp.float32),
            pltpu.VMEM((chaos, dofs), jnp.float32),
            pltpu.SemaphoreType.DMA((2,)),
        ],
        compiler_params=params,
    )(field, all_tiles, tiles, mixer, masks, rhs)

    def partner(s, c):
        return (s + 1) * groups + (c ^ turn ^ 1 if s % RUN == RUN - 1 else c ^ 1)

    pairs = [(s * groups + c, partner(s, c), s) for s in range(slabs - 1) for c in range(groups)]
    axes = ("space", "chaos")

    def swap(x, parity):
        return lax.ppermute(x, axes, [p for a, b, s in pairs if s % 2 == parity for p in ((a, b), (b, a))])

    got_first, got_second = swap(first, 1), swap(second, 0)
    even = (lax.axis_index("space") % 2) == 0
    halo_a = jnp.where(even, got_first, got_second)
    halo_b = jnp.where(even, got_second, got_first)
    got = jnp.concatenate([halo_a, halo_b], axis=1)
    return main - got[:own]


def solution(mesh):
    return jax.shard_map(
        body,
        mesh=mesh,
        in_specs=(
            P("chaos", "space"),
            P(None, "space", None, None, None),
            P("space", None),
            P(),
            P("chaos", "space"),
        ),
        out_specs=P("chaos", "space"),
        check_vma=False,
    )
```

```python
import functools

import jax
import jax.numpy as jnp
from jax import lax
from jax.experimental import pallas as pl
from jax.experimental.pallas import tpu as pltpu
from jax.sharding import PartitionSpec as P

ROWS = 8
REACH = 2
SPAN = 2 * REACH + 1
RUN = 4
BLOCKS = 3


def in_hbm(x):
    return pltpu.with_memory_space_constraint(x, pltpu.HBM)


def split(x):
    high = x.astype(jnp.bfloat16).astype(jnp.float32)
    return high, x - high


def stage_kernel(
    field_ref, offsets_ref, tiles_ref, galerkin_ref,
    copies_out, first_tiles, second_tiles, mixer_out, first_masks, second_masks, own_masks,
    field, offsets, galerkin, mixer, sems,
):
    terms, tile_rows, near, _, _ = tiles_ref.shape
    groups, own, _ = copies_out.shape
    space, block = lax.axis_index("space"), lax.axis_index("chaos")
    odd = lax.rem(space, 2)
    first_row = odd * (tile_rows - REACH)
    second_row = (1 - odd) * (tile_rows - REACH)
    pairs = [(field_ref, field), (galerkin_ref, galerkin), (offsets_ref, offsets)]
    for row, out in ((first_row, first_tiles), (second_row, second_tiles)):
        pairs.append((tiles_ref.at[:, pl.ds(row, REACH), 1:near], out))
    moves = [pltpu.make_async_copy(a, b, sems.at[i]) for i, (a, b) in enumerate(pairs)]
    for move in moves:
        move.start()
    moves[0].wait()
    value = field[...]
    for g in range(groups):
        copies_out[g] = value
    mixer[...] = jnp.zeros_like(mixer)
    moves[1].wait()
    half = groups // 2
    crossed = block + 1 - 2 * lax.rem(block, 2)
    far_off = jnp.where(crossed < half, crossed + half, crossed - half)
    place = lax.rem(space, RUN)
    at_end = jnp.logical_or(place == 0, place == RUN - 1)
    for b, owner in enumerate((jnp.where(at_end, far_off, block), block, block)):
        for k in range(terms):
            mixer[b, k, :own, :] = galerkin[k, pl.ds(owner * own, own), :]
    parts = split(mixer[...].reshape(BLOCKS, terms * ROWS, groups * own))
    mixer_out[...] = jnp.concatenate(parts, axis=1).astype(jnp.bfloat16)
    moves[2].wait()

    def row_of(flag):
        return jnp.full((1, own_masks.shape[1]), flag.astype(jnp.float32))

    for row, out in ((first_row, first_masks), (second_row, second_masks)):
        below = jnp.where(row == 0, -REACH, tile_rows)
        for i in range(REACH):
            for s in range(1, near):
                for t in range(REACH):
                    at = (i * (near - 1) + s - 1) * REACH + t
                    out[at : at + 1, :] = row_of(row + i + offsets[row + i, s] == below + t)
    for r in range(tile_rows):
        for s in range(1, near):
            for t in range(tile_rows):
                at = (r * (near - 1) + s - 1) * tile_rows + t
                own_masks[at : at + 1, :] = row_of(r + offsets[r, s] == t)
    for move in moves[3:]:
        move.wait()


def mix(field_ref, mixer_ref, block, columns, gathered):
    groups, own, _ = field_ref.shape
    rows = mixer_ref.shape[1] // 2
    for g in range(groups):
        gathered[g * own : (g + 1) * own, :] = field_ref[g, :, columns].astype(jnp.float32)
    field = gathered[...].astype(jnp.bfloat16)
    both = jnp.dot(mixer_ref[block], field, preferred_element_type=jnp.float32)
    mixed = (both[:rows] + both[rows:]).reshape(rows // ROWS, ROWS, field.shape[1])
    return split(mixed)


def times_tiles(parts, columns, tiles):
    terms, near, size, _ = tiles.shape
    left = jnp.concatenate(
        [jnp.concatenate([part[k, :, columns] for part in parts], axis=0) for k in range(terms)],
        axis=1,
    ).astype(jnp.bfloat16)
    right = jnp.concatenate([tiles[:, s].reshape(terms * size, size) for s in range(near)], axis=1)
    product = jnp.dot(left, right, preferred_element_type=jnp.float32)
    product = product[:ROWS] + product[ROWS:]
    return [product[:, s * size : (s + 1) * size] for s in range(near)]


def halo_kernel(which, field_ref, tiles_ref, mixer_ref, masks_ref, halo_ref, gathered):
    others, size = tiles_ref.shape[2:4]
    tile_rows = field_ref.shape[2] // size
    odd = lax.rem(lax.axis_index("space"), 2)
    row = (odd if which == 0 else 1 - odd) * (tile_rows - REACH)
    columns = pl.ds(pl.multiple_of(row * size, size), REACH * size)
    parts = mix(field_ref, mixer_ref, which, columns, gathered)
    halos = [jnp.zeros((ROWS, size), jnp.float32) for _ in range(REACH)]
    for i in range(REACH):
        entries = times_tiles(parts, slice(i * size, (i + 1) * size), tiles_ref[:, i])
        for s in range(others):
            for t in range(REACH):
                at = (i * others + s) * REACH + t
                halos[t] += jnp.where(masks_ref[at : at + 1, :] > 0, entries[s], 0.0)
    for t in range(REACH):
        halo_ref[:, t * size : (t + 1) * size] = halos[t]


def own_kernel(
    field_ref, tiles_hbm, mixer_ref, masks_ref, rhs_hbm,
    main_ref, tiles, rhs, gathered, sems,
):
    _, tile_rows, near, size, _ = tiles.shape
    own = field_ref.shape[1]
    get_rhs = pltpu.make_async_copy(rhs_hbm, rhs, sems.at[0])
    get_tiles = [
        pltpu.make_async_copy(tiles_hbm.at[:, r], tiles.at[:, r], sems.at[1 + r])
        for r in range(tile_rows)
    ]
    for move in (*get_tiles, get_rhs):
        move.start()
    parts = mix(field_ref, mixer_ref, BLOCKS - 1, slice(None), gathered)
    sums = [jnp.zeros((ROWS, size), jnp.float32) for _ in range(tile_rows)]
    for r in range(tile_rows):
        get_tiles[r].wait()
        entries = times_tiles(parts, slice(r * size, (r + 1) * size), tiles[:, r])
        sums[r] += entries[0]
        for s in range(1, near):
            for t in range(tile_rows):
                if abs(t - r) > REACH or t == r:
                    continue
                at = (r * (near - 1) + s - 1) * tile_rows + t
                sums[t] += jnp.where(masks_ref[at : at + 1, :] > 0, entries[s], 0.0)
    get_rhs.wait()
    for t in range(tile_rows):
        columns = slice(t * size, (t + 1) * size)
        main_ref[:, columns] = rhs[:, columns] - sums[t][:own]


def body(adjoint_field, stiffness_tiles, offsets, galerkin, adjoint_rhs):
    terms, tile_rows, near, size, _ = stiffness_tiles.shape
    own, dofs = adjoint_field.shape
    groups, slabs = lax.axis_size("chaos"), lax.axis_size("space")
    chaos = own * groups
    turn = groups // 2
    vmem = pl.BlockSpec(memory_space=pltpu.VMEM)
    hbm = pl.BlockSpec(memory_space=pltpu.HBM)
    params = pltpu.CompilerParams(vmem_limit_bytes=24 * 1024 * 1024)
    all_tiles, rhs = in_hbm(stiffness_tiles), in_hbm(adjoint_rhs)

    def floats(*shape):
        return jax.ShapeDtypeStruct(shape, jnp.float32)

    def halves(*shape):
        return jax.ShapeDtypeStruct(shape, jnp.bfloat16)

    side = (terms, REACH, near - 1, size, size)
    side_masks = REACH * (near - 1) * REACH
    copies, first_tiles, second_tiles, mixer, first_masks, second_masks, own_masks = pl.pallas_call(
        stage_kernel,
        out_shape=(
            halves(groups, own, dofs),
            halves(*side),
            halves(*side),
            halves(BLOCKS, 2 * terms * ROWS, chaos),
            floats(side_masks, size),
            floats(side_masks, size),
            floats(tile_rows * (near - 1) * tile_rows, size),
        ),
        in_specs=[hbm] * 4,
        out_specs=(vmem,) * 7,
        scratch_shapes=[
            pltpu.VMEM((own, dofs), jnp.bfloat16),
            pltpu.SMEM(offsets.shape, jnp.int32),
            pltpu.VMEM((terms, chaos, chaos), jnp.float32),
            pltpu.VMEM((BLOCKS, terms, ROWS, chaos), jnp.float32),
            pltpu.SemaphoreType.DMA((5,)),
        ],
        compiler_params=params,
    )(in_hbm(adjoint_field), in_hbm(offsets), all_tiles, in_hbm(galerkin))

    field = lax.all_to_all(copies, "chaos", 0, 0)

    def halo_of(which, tiles, masks):
        return pl.pallas_call(
            functools.partial(halo_kernel, which),
            out_shape=floats(ROWS, REACH * size),
            in_specs=[vmem] * 4,
            out_specs=vmem,
            scratch_shapes=[pltpu.VMEM((chaos, REACH * size), jnp.float32)],
            compiler_params=params,
        )(field, tiles, mixer, masks)

    first = halo_of(0, first_tiles, first_masks)
    second = halo_of(1, second_tiles, second_masks)

    main = pl.pallas_call(
        own_kernel,
        out_shape=floats(own, dofs),
        in_specs=[vmem, hbm, vmem, vmem, hbm],
        out_specs=vmem,
        scratch_shapes=[
            pltpu.VMEM(stiffness_tiles.shape, jnp.bfloat16),
            pltpu.VMEM((own, dofs), jnp.float32),
            pltpu.VMEM((chaos, dofs), jnp.float32),
            pltpu.SemaphoreType.DMA((1 + tile_rows,)),
        ],
        compiler_params=params,
    )(field, all_tiles, mixer, own_masks, rhs)

    def partner(s, c):
        return (s + 1) * groups + (c ^ turn ^ 1 if s % RUN == RUN - 1 else c)

    pairs = [(s * groups + c, partner(s, c), s) for s in range(slabs - 1) for c in range(groups)]
    axes = ("space", "chaos")

    def swap(x, parity):
        return lax.ppermute(x, axes, [p for a, b, s in pairs if s % 2 == parity for p in ((a, b), (b, a))])

    got_first, got_second = swap(first, 1), swap(second, 0)
    even = (lax.axis_index("space") % 2) == 0
    halo_a = jnp.where(even, got_first, got_second)
    halo_b = jnp.where(even, got_second, got_first)
    got = jnp.concatenate([halo_a, halo_b], axis=1)
    return main - got[:own]


def solution(mesh):
    return jax.shard_map(
        body,
        mesh=mesh,
        in_specs=(
            P("chaos", "space"),
            P(None, "space", None, None, None),
            P("space", None),
            P(),
            P("chaos", "space"),
        ),
        out_specs=P("chaos", "space"),
        check_vma=False,
    )
```

```python
import jax
import jax.numpy as jnp
from jax import lax
from jax.experimental import pallas as pl
from jax.experimental.pallas import tpu as pltpu
from jax.sharding import PartitionSpec as P

ROWS = 8
REACH = 2
SPAN = 2 * REACH + 1
RUN = 4
ACROSS = (3, 2, 0, 1)
BLOCKS = 3


def across(c):
    return 2 * ACROSS[c // 2] + 1 - c % 2


def is_late():
    upper = lax.rem(lax.axis_index("space") // RUN, 2)
    return lax.axis_index("chaos") // 2 == (1 - upper) * (lax.axis_size("chaos") // 2 - 1)


def in_hbm(x):
    return pltpu.with_memory_space_constraint(x, pltpu.HBM)


def split(x):
    high = x.astype(jnp.bfloat16).astype(jnp.float32)
    return high, x - high


def moves_of(hbm_refs, staged, scratch, first=0, last=4):
    offsets_hbm, tiles_hbm, galerkin_hbm = hbm_refs
    offsets, galerkin, _, sems = scratch
    tile_rows, near = tiles_hbm.shape[1:3]
    first_row, second_row = side_rows(tile_rows)
    pairs = [(galerkin_hbm, galerkin), (offsets_hbm, offsets)]
    for row, out in zip((first_row, second_row), staged[:2]):
        pairs.append((tiles_hbm.at[:, pl.ds(row, REACH), 1:near], out))
    return [pltpu.make_async_copy(*pairs[i], sems.at[i]) for i in range(first, last)]


def side_rows(tile_rows):
    odd = lax.rem(lax.axis_index("space"), 2)
    return odd * (tile_rows - REACH), (1 - odd) * (tile_rows - REACH)


def stage(hbm_refs, staged, scratch):
    _, _, mixer_out, first_masks, second_masks, own_masks = staged
    offsets, galerkin, mixer, _ = scratch
    moves = moves_of(hbm_refs, staged, scratch, 0, 2)
    terms, tile_rows, near, _, _ = hbm_refs[1].shape
    groups = lax.axis_size("chaos")
    own = galerkin.shape[1] // groups
    space, block = lax.axis_index("space"), lax.axis_index("chaos")
    mixer[...] = jnp.zeros_like(mixer)
    moves[0].wait()
    place = lax.rem(space, RUN)
    at_end = jnp.logical_or(place == 0, place == RUN - 1)
    far_off = block
    for c in range(groups):
        here = jnp.where(place == 0, across(c) == block, c == block)
        far_off = jnp.where(here, jnp.where(place == 0, c, across(c)), far_off)
    for b, owner in enumerate((jnp.where(at_end, far_off, block), block, block)):
        for k in range(terms):
            mixer[b, k, :own, :] = galerkin[k, pl.ds(owner * own, own), :]
    parts = split(mixer[...].reshape(BLOCKS, terms * ROWS, groups * own))
    mixer_out[...] = jnp.concatenate(parts, axis=1).astype(jnp.bfloat16)
    moves[1].wait()

    first_row, second_row = side_rows(tile_rows)

    def row_of(flag):
        return jnp.full((1, own_masks.shape[1]), flag.astype(jnp.float32))

    for row, out in ((first_row, first_masks), (second_row, second_masks)):
        below = jnp.where(row == 0, -REACH, tile_rows)
        for i in range(REACH):
            for s in range(1, near):
                for t in range(REACH):
                    at = (i * (near - 1) + s - 1) * REACH + t
                    out[at : at + 1, :] = row_of(row + i + offsets[row + i, s] == below + t)
    for r in range(tile_rows):
        for s in range(1, near):
            for t in range(tile_rows):
                at = (r * (near - 1) + s - 1) * tile_rows + t
                own_masks[at : at + 1, :] = row_of(r + offsets[r, s] == t)


def stage_kernel(
    field_ref, offsets_hbm, tiles_hbm, galerkin_hbm,
    copies_out, first_tiles, second_tiles, mixer_out, first_masks, second_masks, own_masks,
    offsets, galerkin, mixer, sems, field, field_sem,
):
    hbm_refs = offsets_hbm, tiles_hbm, galerkin_hbm
    staged = first_tiles, second_tiles, mixer_out, first_masks, second_masks, own_masks
    scratch = offsets, galerkin, mixer, sems
    get_field = pltpu.make_async_copy(field_ref, field, field_sem)
    get_field.start()

    @pl.when(jnp.logical_not(is_late()))
    def _():
        for move in moves_of(hbm_refs, staged, scratch):
            move.start()

    get_field.wait()
    value = field[...]
    for g in range(copies_out.shape[0]):
        copies_out[g] = value

    @pl.when(jnp.logical_not(is_late()))
    def _():
        stage(hbm_refs, staged, scratch)
        for move in moves_of(hbm_refs, staged, scratch, 2):
            move.wait()


def mix(field_ref, mixer_ref, block, columns, gathered):
    groups, own, _ = field_ref.shape
    rows = mixer_ref.shape[1] // 2
    for g in range(groups):
        gathered[g * own : (g + 1) * own, :] = field_ref[g, :, columns].astype(jnp.float32)
    field = gathered[...].astype(jnp.bfloat16)
    both = jnp.dot(mixer_ref[block], field, preferred_element_type=jnp.float32)
    mixed = (both[:rows] + both[rows:]).reshape(rows // ROWS, ROWS, field.shape[1])
    return split(mixed)


def times_tiles(parts, columns, tiles):
    terms, near, size, _ = tiles.shape
    left = jnp.concatenate(
        [jnp.concatenate([part[k, :, columns] for part in parts], axis=0) for k in range(terms)],
        axis=1,
    ).astype(jnp.bfloat16)
    right = jnp.concatenate([tiles[:, s].reshape(terms * size, size) for s in range(near)], axis=1)
    product = jnp.dot(left, right, preferred_element_type=jnp.float32)
    product = product[:ROWS] + product[ROWS:]
    return [product[:, s * size : (s + 1) * size] for s in range(near)]


def side_parts(which, field_ref, mixer_ref, size, gathered):
    row = side_rows(field_ref.shape[2] // size)[which]
    columns = pl.ds(pl.multiple_of(row * size, size), REACH * size)
    return mix(field_ref, mixer_ref, which, columns, gathered)


def side_halo(parts, tiles_ref, masks_ref, halo_ref):
    others, size = tiles_ref.shape[2:4]
    halos = [jnp.zeros((ROWS, size), jnp.float32) for _ in range(REACH)]
    for i in range(REACH):
        entries = times_tiles(parts, slice(i * size, (i + 1) * size), tiles_ref[:, i])
        for s in range(others):
            for t in range(REACH):
                at = (i * others + s) * REACH + t
                halos[t] += jnp.where(masks_ref[at : at + 1, :] > 0, entries[s], 0.0)
    for t in range(REACH):
        halo_ref[:, t * size : (t + 1) * size] = halos[t]


def halos_kernel(*refs):
    field_ref, hbm_refs, halo_refs = refs[0], refs[7:10], refs[10:12]
    staged, scratch, gathered = refs[12:18], refs[18:22], refs[22]

    @pl.when(is_late())
    def _():
        for move in moves_of(hbm_refs, staged, scratch):
            move.start()
        stage(hbm_refs, staged, scratch)

    size = staged[0].shape[3]
    parts = [side_parts(which, field_ref, staged[2], size, gathered.at[which]) for which in range(2)]

    @pl.when(is_late())
    def _():
        for move in moves_of(hbm_refs, staged, scratch, 2):
            move.wait()

    for which in range(2):
        side_halo(parts[which], staged[which], staged[3 + which], halo_refs[which])


def own_kernel(
    field_ref, tiles_hbm, mixer_ref, masks_ref, rhs_hbm,
    main_ref, tiles, rhs, gathered, sems,
):
    _, tile_rows, near, size, _ = tiles.shape
    own = field_ref.shape[1]
    get_rhs = pltpu.make_async_copy(rhs_hbm, rhs, sems.at[0])
    get_tiles = [
        pltpu.make_async_copy(tiles_hbm.at[:, r], tiles.at[:, r], sems.at[1 + r])
        for r in range(tile_rows)
    ]
    for move in (*get_tiles, get_rhs):
        move.start()
    parts = mix(field_ref, mixer_ref, BLOCKS - 1, slice(None), gathered)
    sums = [jnp.zeros((ROWS, size), jnp.float32) for _ in range(tile_rows)]
    for r in range(tile_rows):
        get_tiles[r].wait()
        entries = times_tiles(parts, slice(r * size, (r + 1) * size), tiles[:, r])
        sums[r] += entries[0]
        for s in range(1, near):
            for t in range(tile_rows):
                if abs(t - r) > REACH or t == r:
                    continue
                at = (r * (near - 1) + s - 1) * tile_rows + t
                sums[t] += jnp.where(masks_ref[at : at + 1, :] > 0, entries[s], 0.0)
    get_rhs.wait()
    for t in range(tile_rows):
        columns = slice(t * size, (t + 1) * size)
        main_ref[:, columns] = rhs[:, columns] - sums[t][:own]


def body(adjoint_field, stiffness_tiles, offsets, galerkin, adjoint_rhs):
    terms, tile_rows, near, size, _ = stiffness_tiles.shape
    own, dofs = adjoint_field.shape
    groups, slabs = lax.axis_size("chaos"), lax.axis_size("space")
    chaos = own * groups
    vmem = pl.BlockSpec(memory_space=pltpu.VMEM)
    hbm = pl.BlockSpec(memory_space=pltpu.HBM)
    params = pltpu.CompilerParams(vmem_limit_bytes=24 * 1024 * 1024)
    all_tiles, rhs = in_hbm(stiffness_tiles), in_hbm(adjoint_rhs)

    def floats(*shape):
        return jax.ShapeDtypeStruct(shape, jnp.float32)

    def halves(*shape):
        return jax.ShapeDtypeStruct(shape, jnp.bfloat16)

    side = (terms, REACH, near - 1, size, size)
    side_masks = REACH * (near - 1) * REACH
    staged_shapes = (
        halves(*side),
        halves(*side),
        halves(BLOCKS, 2 * terms * ROWS, chaos),
        floats(side_masks, size),
        floats(side_masks, size),
        floats(tile_rows * (near - 1) * tile_rows, size),
    )
    stage_scratch = [
        pltpu.SMEM(offsets.shape, jnp.int32),
        pltpu.VMEM((terms, chaos, chaos), jnp.float32),
        pltpu.VMEM((BLOCKS, terms, ROWS, chaos), jnp.float32),
        pltpu.SemaphoreType.DMA((4,)),
    ]
    sources = in_hbm(offsets), all_tiles, in_hbm(galerkin)
    copies, *staged = pl.pallas_call(
        stage_kernel,
        out_shape=(halves(groups, own, dofs), *staged_shapes),
        in_specs=[hbm] * 4,
        out_specs=(vmem,) * 7,
        scratch_shapes=[*stage_scratch, pltpu.VMEM((own, dofs), jnp.bfloat16), pltpu.SemaphoreType.DMA],
        compiler_params=params,
    )(in_hbm(adjoint_field), *sources)

    field = lax.all_to_all(copies, "chaos", 0, 0)

    halo = floats(ROWS, REACH * size)
    first, second, *staged = pl.pallas_call(
        halos_kernel,
        out_shape=(halo, halo, *staged_shapes),
        in_specs=[vmem] * 7 + [hbm] * 3,
        out_specs=(vmem,) * 8,
        input_output_aliases={1 + i: 2 + i for i in range(6)},
        scratch_shapes=[*stage_scratch, pltpu.VMEM((2, chaos, REACH * size), jnp.float32)],
        compiler_params=params,
    )(field, *staged, *sources)
    mixer, own_masks = staged[2], staged[5]

    main = pl.pallas_call(
        own_kernel,
        out_shape=floats(own, dofs),
        in_specs=[vmem, hbm, vmem, vmem, hbm],
        out_specs=vmem,
        scratch_shapes=[
            pltpu.VMEM(stiffness_tiles.shape, jnp.bfloat16),
            pltpu.VMEM((own, dofs), jnp.float32),
            pltpu.VMEM((chaos, dofs), jnp.float32),
            pltpu.SemaphoreType.DMA((1 + tile_rows,)),
        ],
        compiler_params=params,
    )(field, all_tiles, mixer, own_masks, rhs)

    def partner(s, c):
        return (s + 1) * groups + (across(c) if s % RUN == RUN - 1 else c)

    pairs = [(s * groups + c, partner(s, c), s) for s in range(slabs - 1) for c in range(groups)]
    axes = ("space", "chaos")

    def swap(x, parity):
        return lax.ppermute(x, axes, [p for a, b, s in pairs if s % 2 == parity for p in ((a, b), (b, a))])

    got_first, got_second = swap(first, 1), swap(second, 0)
    even = (lax.axis_index("space") % 2) == 0
    halo_a = jnp.where(even, got_first, got_second)
    halo_b = jnp.where(even, got_second, got_first)
    got = jnp.concatenate([halo_a, halo_b], axis=1)
    return main - got[:own]


def solution(mesh):
    return jax.shard_map(
        body,
        mesh=mesh,
        in_specs=(
            P("chaos", "space"),
            P(None, "space", None, None, None),
            P("space", None),
            P(),
            P("chaos", "space"),
        ),
        out_specs=P("chaos", "space"),
        check_vma=False,
    )
```

```python
import jax
import jax.numpy as jnp
from jax import lax
from jax.experimental import pallas as pl
from jax.experimental.pallas import tpu as pltpu
from jax.sharding import PartitionSpec as P

ROWS = 8
REACH = 2
SPAN = 2 * REACH + 1
RUN = 4
ACROSS = (3, 2, 0, 1)
BLOCKS = 3


def across(c):
    return 2 * ACROSS[c // 2] + 1 - c % 2


def is_late():
    upper = lax.rem(lax.axis_index("space") // RUN, 2)
    return lax.axis_index("chaos") // 2 == (1 - upper) * (lax.axis_size("chaos") // 2 - 1)


def in_vmem(x):
    return pltpu.with_memory_space_constraint(x, pltpu.VMEM)


def in_hbm(x):
    return pltpu.with_memory_space_constraint(x, pltpu.HBM)


def split(x):
    high = x.astype(jnp.bfloat16).astype(jnp.float32)
    return high, x - high


def moves_of(hbm_refs, staged, scratch, first=0, last=4):
    offsets_hbm, tiles_hbm, galerkin_hbm = hbm_refs
    offsets, galerkin, _, sems = scratch
    tile_rows, near = tiles_hbm.shape[1:3]
    first_row, second_row = side_rows(tile_rows)
    pairs = [(galerkin_hbm, galerkin), (offsets_hbm, offsets)]
    for row, out in zip((first_row, second_row), staged[:2]):
        pairs.append((tiles_hbm.at[:, pl.ds(row, REACH), 1:near], out))
    return [pltpu.make_async_copy(*pairs[i], sems.at[i]) for i in range(first, last)]


def side_rows(tile_rows):
    odd = lax.rem(lax.axis_index("space"), 2)
    return odd * (tile_rows - REACH), (1 - odd) * (tile_rows - REACH)


def stage(hbm_refs, staged, scratch):
    _, _, mixer_out, first_masks, second_masks, own_masks = staged
    offsets, galerkin, mixer, _ = scratch
    moves = moves_of(hbm_refs, staged, scratch, 0, 2)
    terms, tile_rows, near, _, _ = hbm_refs[1].shape
    groups = lax.axis_size("chaos")
    own = galerkin.shape[1] // groups
    space, block = lax.axis_index("space"), lax.axis_index("chaos")
    mixer[...] = jnp.zeros_like(mixer)
    moves[0].wait()
    place = lax.rem(space, RUN)
    at_end = jnp.logical_or(place == 0, place == RUN - 1)
    far_off = block
    for c in range(groups):
        here = jnp.where(place == 0, across(c) == block, c == block)
        far_off = jnp.where(here, jnp.where(place == 0, c, across(c)), far_off)
    for b, owner in enumerate((jnp.where(at_end, far_off, block), block, block)):
        for k in range(terms):
            mixer[b, k, :own, :] = galerkin[k, pl.ds(owner * own, own), :]
    parts = split(mixer[...].reshape(BLOCKS, terms * ROWS, groups * own))
    mixer_out[...] = jnp.concatenate(parts, axis=1).astype(jnp.bfloat16)
    moves[1].wait()

    first_row, second_row = side_rows(tile_rows)

    def row_of(flag):
        return jnp.full((1, own_masks.shape[1]), flag.astype(jnp.float32))

    for row, out in ((first_row, first_masks), (second_row, second_masks)):
        below = jnp.where(row == 0, -REACH, tile_rows)
        for i in range(REACH):
            for s in range(1, near):
                for t in range(REACH):
                    at = (i * (near - 1) + s - 1) * REACH + t
                    out[at : at + 1, :] = row_of(row + i + offsets[row + i, s] == below + t)
    for r in range(tile_rows):
        for s in range(1, near):
            for t in range(tile_rows):
                at = (r * (near - 1) + s - 1) * tile_rows + t
                own_masks[at : at + 1, :] = row_of(r + offsets[r, s] == t)


def stage_kernel(
    field_ref, offsets_hbm, tiles_hbm, galerkin_hbm,
    copies_out, first_tiles, second_tiles, mixer_out, first_masks, second_masks, own_masks,
    offsets, galerkin, mixer, sems, field, field_sem,
):
    hbm_refs = offsets_hbm, tiles_hbm, galerkin_hbm
    staged = first_tiles, second_tiles, mixer_out, first_masks, second_masks, own_masks
    scratch = offsets, galerkin, mixer, sems
    get_field = pltpu.make_async_copy(field_ref, field, field_sem)
    get_field.start()

    @pl.when(jnp.logical_not(is_late()))
    def _():
        for move in moves_of(hbm_refs, staged, scratch):
            move.start()

    get_field.wait()
    value = field[...]
    for g in range(copies_out.shape[0]):
        copies_out[g] = value

    @pl.when(jnp.logical_not(is_late()))
    def _():
        stage(hbm_refs, staged, scratch)
        for move in moves_of(hbm_refs, staged, scratch, 2):
            move.wait()


def mix(field_ref, mixer_ref, block, columns, gathered):
    groups, own, _ = field_ref.shape
    rows = mixer_ref.shape[1] // 2
    for g in range(groups):
        gathered[g * own : (g + 1) * own, :] = field_ref[g, :, columns].astype(jnp.float32)
    field = gathered[...].astype(jnp.bfloat16)
    both = jnp.dot(mixer_ref[block], field, preferred_element_type=jnp.float32)
    mixed = (both[:rows] + both[rows:]).reshape(rows // ROWS, ROWS, field.shape[1])
    return split(mixed)


def times_tiles(parts, columns, tiles):
    terms, near, size, _ = tiles.shape
    left = jnp.concatenate(
        [jnp.concatenate([part[k, :, columns] for part in parts], axis=0) for k in range(terms)],
        axis=1,
    ).astype(jnp.bfloat16)
    right = jnp.concatenate([tiles[:, s].reshape(terms * size, size) for s in range(near)], axis=1)
    product = jnp.dot(left, right, preferred_element_type=jnp.float32)
    product = product[:ROWS] + product[ROWS:]
    return [product[:, s * size : (s + 1) * size] for s in range(near)]


def side_parts(which, field_ref, mixer_ref, size, gathered):
    row = side_rows(field_ref.shape[2] // size)[which]
    columns = pl.ds(pl.multiple_of(row * size, size), REACH * size)
    return mix(field_ref, mixer_ref, which, columns, gathered)


def side_halo(parts, tiles_ref, masks_ref, halo_ref):
    others, size = tiles_ref.shape[2:4]
    halos = [jnp.zeros((ROWS, size), jnp.float32) for _ in range(REACH)]
    for i in range(REACH):
        entries = times_tiles(parts, slice(i * size, (i + 1) * size), tiles_ref[:, i])
        for s in range(others):
            for t in range(REACH):
                at = (i * others + s) * REACH + t
                halos[t] += jnp.where(masks_ref[at : at + 1, :] > 0, entries[s], 0.0)
    for t in range(REACH):
        halo_ref[:, t * size : (t + 1) * size] = halos[t]


def halos_kernel(*refs):
    field_ref, hbm_refs, halo_refs = refs[0], refs[7:10], refs[10:12]
    staged, scratch, gathered = refs[12:18], refs[18:22], refs[22]

    @pl.when(is_late())
    def _():
        for move in moves_of(hbm_refs, staged, scratch):
            move.start()
        stage(hbm_refs, staged, scratch)

    size = staged[0].shape[3]
    parts = [side_parts(which, field_ref, staged[2], size, gathered.at[which]) for which in range(2)]

    @pl.when(is_late())
    def _():
        for move in moves_of(hbm_refs, staged, scratch, 2):
            move.wait()

    for which in range(2):
        side_halo(parts[which], staged[which], staged[3 + which], halo_refs[which])


def own_kernel(
    field_ref, tiles_hbm, mixer_ref, masks_ref, rhs_hbm,
    main_ref, tiles, rhs, gathered, sems,
):
    _, tile_rows, near, size, _ = tiles.shape
    own = field_ref.shape[1]
    get_rhs = pltpu.make_async_copy(rhs_hbm, rhs, sems.at[0])
    get_tiles = [
        pltpu.make_async_copy(tiles_hbm.at[:, r], tiles.at[:, r], sems.at[1 + r])
        for r in range(tile_rows)
    ]
    for move in (*get_tiles, get_rhs):
        move.start()
    parts = mix(field_ref, mixer_ref, BLOCKS - 1, slice(None), gathered)
    sums = [jnp.zeros((ROWS, size), jnp.float32) for _ in range(tile_rows)]
    for r in range(tile_rows):
        get_tiles[r].wait()
        entries = times_tiles(parts, slice(r * size, (r + 1) * size), tiles[:, r])
        sums[r] += entries[0]
        for s in range(1, near):
            for t in range(tile_rows):
                if abs(t - r) > REACH or t == r:
                    continue
                at = (r * (near - 1) + s - 1) * tile_rows + t
                sums[t] += jnp.where(masks_ref[at : at + 1, :] > 0, entries[s], 0.0)
    get_rhs.wait()
    for t in range(tile_rows):
        columns = slice(t * size, (t + 1) * size)
        main_ref[:, columns] = rhs[:, columns] - sums[t][:own]


def body(adjoint_field, stiffness_tiles, offsets, galerkin, adjoint_rhs):
    terms, tile_rows, near, size, _ = stiffness_tiles.shape
    own, dofs = adjoint_field.shape
    groups, slabs = lax.axis_size("chaos"), lax.axis_size("space")
    chaos = own * groups
    vmem = pl.BlockSpec(memory_space=pltpu.VMEM)
    hbm = pl.BlockSpec(memory_space=pltpu.HBM)
    params = pltpu.CompilerParams(vmem_limit_bytes=24 * 1024 * 1024)
    all_tiles, rhs = in_hbm(stiffness_tiles), in_hbm(adjoint_rhs)

    def floats(*shape):
        return jax.ShapeDtypeStruct(shape, jnp.float32)

    def halves(*shape):
        return jax.ShapeDtypeStruct(shape, jnp.bfloat16)

    side = (terms, REACH, near - 1, size, size)
    side_masks = REACH * (near - 1) * REACH
    staged_shapes = (
        pltpu.VMEM(side, jnp.bfloat16),
        pltpu.VMEM(side, jnp.bfloat16),
        pltpu.VMEM((BLOCKS, 2 * terms * ROWS, chaos), jnp.bfloat16),
        pltpu.VMEM((side_masks, size), jnp.float32),
        pltpu.VMEM((side_masks, size), jnp.float32),
        pltpu.VMEM((tile_rows * (near - 1) * tile_rows, size), jnp.float32),
    )
    stage_scratch = [
        pltpu.SMEM(offsets.shape, jnp.int32),
        pltpu.VMEM((terms, chaos, chaos), jnp.float32),
        pltpu.VMEM((BLOCKS, terms, ROWS, chaos), jnp.float32),
        pltpu.SemaphoreType.DMA((4,)),
    ]
    sources = in_hbm(offsets), all_tiles, in_hbm(galerkin)
    copies, *staged = pl.pallas_call(
        stage_kernel,
        out_shape=(halves(groups, own, dofs), *staged_shapes),
        in_specs=[hbm] * 4,
        out_specs=(vmem,) * 7,
        scratch_shapes=[*stage_scratch, pltpu.VMEM((own, dofs), jnp.bfloat16), pltpu.SemaphoreType.DMA],
        compiler_params=params,
    )(in_hbm(adjoint_field), *sources)

    field = lax.all_to_all(copies, "chaos", 0, 0)

    halo = floats(ROWS, REACH * size)
    first, second, *staged = pl.pallas_call(
        halos_kernel,
        out_shape=(halo, halo, *staged_shapes),
        in_specs=[vmem] * 7 + [hbm] * 3,
        out_specs=(vmem,) * 8,
        input_output_aliases={1 + i: 2 + i for i in range(6)},
        scratch_shapes=[*stage_scratch, pltpu.VMEM((2, chaos, REACH * size), jnp.float32)],
        compiler_params=params,
    )(field, *map(in_vmem, staged), *sources)
    mixer, own_masks = staged[2], staged[5]

    main = pl.pallas_call(
        own_kernel,
        out_shape=floats(own, dofs),
        in_specs=[vmem, hbm, vmem, vmem, hbm],
        out_specs=vmem,
        scratch_shapes=[
            pltpu.VMEM(stiffness_tiles.shape, jnp.bfloat16),
            pltpu.VMEM((own, dofs), jnp.float32),
            pltpu.VMEM((chaos, dofs), jnp.float32),
            pltpu.SemaphoreType.DMA((1 + tile_rows,)),
        ],
        compiler_params=params,
    )(field, all_tiles, mixer, own_masks, rhs)

    def partner(s, c):
        return (s + 1) * groups + (across(c) if s % RUN == RUN - 1 else c)

    pairs = [(s * groups + c, partner(s, c), s) for s in range(slabs - 1) for c in range(groups)]
    axes = ("space", "chaos")

    def swap(x, parity):
        return lax.ppermute(x, axes, [p for a, b, s in pairs if s % 2 == parity for p in ((a, b), (b, a))])

    got_first, got_second = swap(first, 1), swap(second, 0)
    even = (lax.axis_index("space") % 2) == 0
    halo_a = jnp.where(even, got_first, got_second)
    halo_b = jnp.where(even, got_second, got_first)
    got = jnp.concatenate([halo_a, halo_b], axis=1)
    return main - got[:own]


def solution(mesh):
    return jax.shard_map(
        body,
        mesh=mesh,
        in_specs=(
            P("chaos", "space"),
            P(None, "space", None, None, None),
            P("space", None),
            P(),
            P("chaos", "space"),
        ),
        out_specs=P("chaos", "space"),
        check_vma=False,
    )
```

```python
import jax
import jax.numpy as jnp
from jax import lax
from jax.experimental import pallas as pl
from jax.experimental.pallas import tpu as pltpu
from jax.sharding import PartitionSpec as P

ROWS = 8
REACH = 2
SPAN = 2 * REACH + 1
RUN = 4
ACROSS = (3, 2, 0, 1)
BLOCKS = 3


def across(c):
    return 2 * ACROSS[c // 2] + 1 - c % 2


def is_late():
    upper = lax.rem(lax.axis_index("space") // RUN, 2)
    return lax.axis_index("chaos") // 2 == (1 - upper) * (lax.axis_size("chaos") // 2 - 1)


def in_vmem(x):
    return pltpu.with_memory_space_constraint(x, pltpu.VMEM)


def in_hbm(x):
    return pltpu.with_memory_space_constraint(x, pltpu.HBM)


def split(x):
    high = x.astype(jnp.bfloat16).astype(jnp.float32)
    return high, x - high


def moves_of(hbm_refs, staged, scratch, first=0, last=4):
    offsets_hbm, tiles_hbm, galerkin_hbm = hbm_refs
    offsets, galerkin, _, sems = scratch
    tile_rows, near = tiles_hbm.shape[1:3]
    first_row, second_row = side_rows(tile_rows)
    pairs = [(galerkin_hbm, galerkin), (offsets_hbm, offsets)]
    for row, out in zip((first_row, second_row), staged[:2]):
        pairs.append((tiles_hbm.at[:, pl.ds(row, REACH), 1:near], out))
    return [pltpu.make_async_copy(*pairs[i], sems.at[i]) for i in range(first, last)]


def side_rows(tile_rows):
    odd = lax.rem(lax.axis_index("space"), 2)
    return odd * (tile_rows - REACH), (1 - odd) * (tile_rows - REACH)


def stage(hbm_refs, staged, scratch):
    _, _, mixer_out, first_masks, second_masks, own_masks = staged
    offsets, galerkin, mixer, _ = scratch
    moves = moves_of(hbm_refs, staged, scratch, 0, 2)
    terms, tile_rows, near, _, _ = hbm_refs[1].shape
    groups = lax.axis_size("chaos")
    own = galerkin.shape[1] // groups
    space, block = lax.axis_index("space"), lax.axis_index("chaos")
    mixer[...] = jnp.zeros_like(mixer)
    moves[0].wait()
    place = lax.rem(space, RUN)
    at_end = jnp.logical_or(place == 0, place == RUN - 1)
    far_off = block
    for c in range(groups):
        here = jnp.where(place == 0, across(c) == block, c == block)
        far_off = jnp.where(here, jnp.where(place == 0, c, across(c)), far_off)
    for b, owner in enumerate((jnp.where(at_end, far_off, block), block, block)):
        for k in range(terms):
            mixer[b, k, :own, :] = galerkin[k, pl.ds(owner * own, own), :]
    parts = split(mixer[...].reshape(BLOCKS, terms * ROWS, groups * own))
    mixer_out[...] = jnp.concatenate(parts, axis=1).astype(jnp.bfloat16)
    moves[1].wait()

    first_row, second_row = side_rows(tile_rows)

    def row_of(flag):
        return jnp.full((1, own_masks.shape[1]), flag.astype(jnp.float32))

    for row, out in ((first_row, first_masks), (second_row, second_masks)):
        below = jnp.where(row == 0, -REACH, tile_rows)
        for i in range(REACH):
            for s in range(1, near):
                for t in range(REACH):
                    at = (i * (near - 1) + s - 1) * REACH + t
                    out[at : at + 1, :] = row_of(row + i + offsets[row + i, s] == below + t)
    for r in range(tile_rows):
        for s in range(1, near):
            for t in range(tile_rows):
                at = (r * (near - 1) + s - 1) * tile_rows + t
                own_masks[at : at + 1, :] = row_of(r + offsets[r, s] == t)


def stage_kernel(
    field_ref, offsets_hbm, tiles_hbm, galerkin_hbm,
    copies_out, first_tiles, second_tiles, mixer_out, first_masks, second_masks, own_masks,
    offsets, galerkin, mixer, sems, field, field_sem,
):
    hbm_refs = offsets_hbm, tiles_hbm, galerkin_hbm
    staged = first_tiles, second_tiles, mixer_out, first_masks, second_masks, own_masks
    scratch = offsets, galerkin, mixer, sems
    get_field = pltpu.make_async_copy(field_ref, field, field_sem)
    get_field.start()

    @pl.when(jnp.logical_not(is_late()))
    def _():
        for move in moves_of(hbm_refs, staged, scratch):
            move.start()

    get_field.wait()
    value = field[...]
    for g in range(copies_out.shape[0]):
        copies_out[g] = value

    @pl.when(jnp.logical_not(is_late()))
    def _():
        stage(hbm_refs, staged, scratch)
        for move in moves_of(hbm_refs, staged, scratch, 2):
            move.wait()


def mix(field_ref, mixer_ref, block, columns, gathered):
    groups, own, _ = field_ref.shape
    rows = mixer_ref.shape[1] // 2
    for g in range(groups):
        gathered[g * own : (g + 1) * own, :] = field_ref[g, :, columns].astype(jnp.float32)
    field = gathered[...].astype(jnp.bfloat16)
    both = jnp.dot(mixer_ref[block], field, preferred_element_type=jnp.float32)
    mixed = (both[:rows] + both[rows:]).reshape(rows // ROWS, ROWS, field.shape[1])
    return split(mixed)


def times_tiles(parts, columns, tiles):
    terms, near, size, _ = tiles.shape
    left = jnp.concatenate(
        [jnp.concatenate([part[k, :, columns] for part in parts], axis=0) for k in range(terms)],
        axis=1,
    ).astype(jnp.bfloat16)
    right = jnp.concatenate([tiles[:, s].reshape(terms * size, size) for s in range(near)], axis=1)
    product = jnp.dot(left, right, preferred_element_type=jnp.float32)
    product = product[:ROWS] + product[ROWS:]
    return [product[:, s * size : (s + 1) * size] for s in range(near)]


def side_parts(which, field_ref, mixer_ref, size, gathered):
    row = side_rows(field_ref.shape[2] // size)[which]
    columns = pl.ds(pl.multiple_of(row * size, size), REACH * size)
    return mix(field_ref, mixer_ref, which, columns, gathered)


def side_halo(parts, tiles_ref, masks_ref, halo_ref):
    others, size = tiles_ref.shape[2:4]
    halos = [jnp.zeros((ROWS, size), jnp.float32) for _ in range(REACH)]
    for i in range(REACH):
        entries = times_tiles(parts, slice(i * size, (i + 1) * size), tiles_ref[:, i])
        for s in range(others):
            for t in range(REACH):
                at = (i * others + s) * REACH + t
                halos[t] += jnp.where(masks_ref[at : at + 1, :] > 0, entries[s], 0.0)
    for t in range(REACH):
        halo_ref[:, t * size : (t + 1) * size] = halos[t]


def halos_kernel(*refs):
    field_ref, hbm_refs, halo_refs = refs[0], refs[7:10], refs[10:12]
    staged, scratch, gathered = refs[12:18], refs[18:22], refs[22]

    size = staged[0].shape[3]

    def make_halos(ready):
        parts = [side_parts(which, field_ref, staged[2], size, gathered.at[which]) for which in range(2)]
        for which in range(2):
            ready(which)
            side_halo(parts[which], staged[which], staged[3 + which], halo_refs[which])

    @pl.when(is_late())
    def _():
        for move in moves_of(hbm_refs, staged, scratch):
            move.start()
        stage(hbm_refs, staged, scratch)

        def ready(which):
            for move in moves_of(hbm_refs, staged, scratch, 2 + which, 3 + which):
                move.wait()

        make_halos(ready)

    @pl.when(jnp.logical_not(is_late()))
    def _():
        make_halos(lambda which: None)


def own_kernel(
    field_ref, tiles_hbm, mixer_ref, masks_ref, rhs_hbm,
    main_ref, tiles, rhs, gathered, sems,
):
    _, tile_rows, near, size, _ = tiles.shape
    own = field_ref.shape[1]
    get_rhs = pltpu.make_async_copy(rhs_hbm, rhs, sems.at[0])
    get_tiles = [
        pltpu.make_async_copy(tiles_hbm.at[:, r], tiles.at[:, r], sems.at[1 + r])
        for r in range(tile_rows)
    ]
    for move in (*get_tiles, get_rhs):
        move.start()
    parts = mix(field_ref, mixer_ref, BLOCKS - 1, slice(None), gathered)
    sums = [jnp.zeros((ROWS, size), jnp.float32) for _ in range(tile_rows)]
    for r in range(tile_rows):
        get_tiles[r].wait()
        entries = times_tiles(parts, slice(r * size, (r + 1) * size), tiles[:, r])
        sums[r] += entries[0]
        for s in range(1, near):
            for t in range(tile_rows):
                if abs(t - r) > REACH or t == r:
                    continue
                at = (r * (near - 1) + s - 1) * tile_rows + t
                sums[t] += jnp.where(masks_ref[at : at + 1, :] > 0, entries[s], 0.0)
    get_rhs.wait()
    for t in range(tile_rows):
        columns = slice(t * size, (t + 1) * size)
        main_ref[:, columns] = rhs[:, columns] - sums[t][:own]


def body(adjoint_field, stiffness_tiles, offsets, galerkin, adjoint_rhs):
    terms, tile_rows, near, size, _ = stiffness_tiles.shape
    own, dofs = adjoint_field.shape
    groups, slabs = lax.axis_size("chaos"), lax.axis_size("space")
    chaos = own * groups
    vmem = pl.BlockSpec(memory_space=pltpu.VMEM)
    hbm = pl.BlockSpec(memory_space=pltpu.HBM)
    params = pltpu.CompilerParams(vmem_limit_bytes=24 * 1024 * 1024)
    all_tiles, rhs = in_hbm(stiffness_tiles), in_hbm(adjoint_rhs)

    def floats(*shape):
        return jax.ShapeDtypeStruct(shape, jnp.float32)

    def halves(*shape):
        return jax.ShapeDtypeStruct(shape, jnp.bfloat16)

    side = (terms, REACH, near - 1, size, size)
    side_masks = REACH * (near - 1) * REACH
    staged_shapes = (
        pltpu.VMEM(side, jnp.bfloat16),
        pltpu.VMEM(side, jnp.bfloat16),
        pltpu.VMEM((BLOCKS, 2 * terms * ROWS, chaos), jnp.bfloat16),
        pltpu.VMEM((side_masks, size), jnp.float32),
        pltpu.VMEM((side_masks, size), jnp.float32),
        pltpu.VMEM((tile_rows * (near - 1) * tile_rows, size), jnp.float32),
    )
    stage_scratch = [
        pltpu.SMEM(offsets.shape, jnp.int32),
        pltpu.VMEM((terms, chaos, chaos), jnp.float32),
        pltpu.VMEM((BLOCKS, terms, ROWS, chaos), jnp.float32),
        pltpu.SemaphoreType.DMA((4,)),
    ]
    sources = in_hbm(offsets), all_tiles, in_hbm(galerkin)
    copies, *staged = pl.pallas_call(
        stage_kernel,
        out_shape=(halves(groups, own, dofs), *staged_shapes),
        in_specs=[hbm] * 4,
        out_specs=(vmem,) * 7,
        scratch_shapes=[*stage_scratch, pltpu.VMEM((own, dofs), jnp.bfloat16), pltpu.SemaphoreType.DMA],
        compiler_params=params,
    )(in_hbm(adjoint_field), *sources)

    field = lax.all_to_all(copies, "chaos", 0, 0)

    halo = floats(ROWS, REACH * size)
    first, second, *staged = pl.pallas_call(
        halos_kernel,
        out_shape=(halo, halo, *staged_shapes),
        in_specs=[vmem] * 7 + [hbm] * 3,
        out_specs=(vmem,) * 8,
        input_output_aliases={1 + i: 2 + i for i in range(6)},
        scratch_shapes=[*stage_scratch, pltpu.VMEM((2, chaos, REACH * size), jnp.float32)],
        compiler_params=params,
    )(field, *map(in_vmem, staged), *sources)
    mixer, own_masks = staged[2], staged[5]

    main = pl.pallas_call(
        own_kernel,
        out_shape=floats(own, dofs),
        in_specs=[vmem, hbm, vmem, vmem, hbm],
        out_specs=vmem,
        scratch_shapes=[
            pltpu.VMEM(stiffness_tiles.shape, jnp.bfloat16),
            pltpu.VMEM((own, dofs), jnp.float32),
            pltpu.VMEM((chaos, dofs), jnp.float32),
            pltpu.SemaphoreType.DMA((1 + tile_rows,)),
        ],
        compiler_params=params,
    )(field, all_tiles, mixer, own_masks, rhs)

    def partner(s, c):
        return (s + 1) * groups + (across(c) if s % RUN == RUN - 1 else c)

    pairs = [(s * groups + c, partner(s, c), s) for s in range(slabs - 1) for c in range(groups)]
    axes = ("space", "chaos")

    def swap(x, parity):
        return lax.ppermute(x, axes, [p for a, b, s in pairs if s % 2 == parity for p in ((a, b), (b, a))])

    got_first, got_second = swap(first, 1), swap(second, 0)
    even = (lax.axis_index("space") % 2) == 0
    halo_a = jnp.where(even, got_first, got_second)
    halo_b = jnp.where(even, got_second, got_first)
    got = jnp.concatenate([halo_a, halo_b], axis=1)
    return main - got[:own]


def solution(mesh):
    return jax.shard_map(
        body,
        mesh=mesh,
        in_specs=(
            P("chaos", "space"),
            P(None, "space", None, None, None),
            P("space", None),
            P(),
            P("chaos", "space"),
        ),
        out_specs=P("chaos", "space"),
        check_vma=False,
    )
```

```python
import jax
import jax.numpy as jnp
from jax import lax
from jax.experimental import pallas as pl
from jax.experimental.pallas import tpu as pltpu
from jax.sharding import PartitionSpec as P

ROWS = 8
REACH = 2
SPAN = 2 * REACH + 1
RUN = 4
ACROSS = (3, 2, 0, 1)
SIDES = 2


def across(c):
    return 2 * ACROSS[c // 2] + 1 - c % 2


def is_late():
    upper = lax.rem(lax.axis_index("space") // RUN, 2)
    return lax.axis_index("chaos") // 2 == (1 - upper) * (lax.axis_size("chaos") // 2 - 1)


def in_vmem(x):
    return pltpu.with_memory_space_constraint(x, pltpu.VMEM)


def in_hbm(x):
    return pltpu.with_memory_space_constraint(x, pltpu.HBM)


def split(x):
    high = x.astype(jnp.bfloat16).astype(jnp.float32)
    return high, x - high


def moves_of(hbm_refs, staged, scratch, first=0, last=4):
    offsets_hbm, tiles_hbm, galerkin_hbm = hbm_refs
    offsets, galerkin, _, sems = scratch
    tile_rows, near = tiles_hbm.shape[1:3]
    first_row, second_row = side_rows(tile_rows)
    pairs = [(galerkin_hbm, galerkin), (offsets_hbm, offsets)]
    for row, out in zip((first_row, second_row), staged[:2]):
        pairs.append((tiles_hbm.at[:, pl.ds(row, REACH), 1:near], out))
    return [pltpu.make_async_copy(*pairs[i], sems.at[i]) for i in range(first, last)]


def side_rows(tile_rows):
    odd = lax.rem(lax.axis_index("space"), 2)
    return odd * (tile_rows - REACH), (1 - odd) * (tile_rows - REACH)


def set_mixer(mixer_out, galerkin, mixer, owners):
    terms = galerkin.shape[0]
    own = galerkin.shape[1] // lax.axis_size("chaos")
    mixer[...] = jnp.zeros_like(mixer)
    for b, owner in enumerate(owners):
        for k in range(terms):
            mixer[b, k, :own, :] = galerkin[k, pl.ds(owner * own, own), :]
    parts = split(mixer[...].reshape(len(owners), terms * ROWS, galerkin.shape[1]))
    mixer_out[...] = jnp.concatenate(parts, axis=1).astype(jnp.bfloat16)


def stage(hbm_refs, staged, scratch):
    _, _, mixer_out, first_masks, second_masks = staged
    offsets, galerkin, mixer, _ = scratch
    moves = moves_of(hbm_refs, staged, scratch, 0, 2)
    tile_rows, near = hbm_refs[1].shape[1:3]
    groups = lax.axis_size("chaos")
    space, block = lax.axis_index("space"), lax.axis_index("chaos")
    moves[0].wait()
    place = lax.rem(space, RUN)
    at_end = jnp.logical_or(place == 0, place == RUN - 1)
    far_off = block
    for c in range(groups):
        here = jnp.where(place == 0, across(c) == block, c == block)
        far_off = jnp.where(here, jnp.where(place == 0, c, across(c)), far_off)
    set_mixer(mixer_out, galerkin, mixer, (jnp.where(at_end, far_off, block), block))
    moves[1].wait()

    first_row, second_row = side_rows(tile_rows)

    def row_of(flag):
        return jnp.full((1, first_masks.shape[1]), flag.astype(jnp.float32))

    for row, out in ((first_row, first_masks), (second_row, second_masks)):
        below = jnp.where(row == 0, -REACH, tile_rows)
        for i in range(REACH):
            for s in range(1, near):
                for t in range(REACH):
                    at = (i * (near - 1) + s - 1) * REACH + t
                    out[at : at + 1, :] = row_of(row + i + offsets[row + i, s] == below + t)


def stage_kernel(
    field_ref, offsets_hbm, tiles_hbm, galerkin_hbm,
    copies_out, first_tiles, second_tiles, mixer_out, first_masks, second_masks,
    offsets, galerkin, mixer, sems, field, field_sem,
):
    hbm_refs = offsets_hbm, tiles_hbm, galerkin_hbm
    staged = first_tiles, second_tiles, mixer_out, first_masks, second_masks
    scratch = offsets, galerkin, mixer, sems
    get_field = pltpu.make_async_copy(field_ref, field, field_sem)
    get_field.start()

    @pl.when(jnp.logical_not(is_late()))
    def _():
        for move in moves_of(hbm_refs, staged, scratch):
            move.start()

    get_field.wait()
    value = field[...]
    for g in range(copies_out.shape[0]):
        copies_out[g] = value

    @pl.when(jnp.logical_not(is_late()))
    def _():
        stage(hbm_refs, staged, scratch)
        for move in moves_of(hbm_refs, staged, scratch, 2):
            move.wait()


def mix(field_ref, mixer_ref, block, columns, gathered):
    groups, own, _ = field_ref.shape
    rows = mixer_ref.shape[1] // 2
    for g in range(groups):
        gathered[g * own : (g + 1) * own, :] = field_ref[g, :, columns].astype(jnp.float32)
    field = gathered[...].astype(jnp.bfloat16)
    both = jnp.dot(mixer_ref[block], field, preferred_element_type=jnp.float32)
    mixed = (both[:rows] + both[rows:]).reshape(rows // ROWS, ROWS, field.shape[1])
    return split(mixed)


def times_tiles(parts, columns, tiles):
    terms, near, size, _ = tiles.shape
    left = jnp.concatenate(
        [jnp.concatenate([part[k, :, columns] for part in parts], axis=0) for k in range(terms)],
        axis=1,
    ).astype(jnp.bfloat16)
    right = jnp.concatenate([tiles[:, s].reshape(terms * size, size) for s in range(near)], axis=1)
    product = jnp.dot(left, right, preferred_element_type=jnp.float32)
    product = product[:ROWS] + product[ROWS:]
    return [product[:, s * size : (s + 1) * size] for s in range(near)]


def side_parts(which, field_ref, mixer_ref, size, gathered):
    row = side_rows(field_ref.shape[2] // size)[which]
    columns = pl.ds(pl.multiple_of(row * size, size), REACH * size)
    return mix(field_ref, mixer_ref, which, columns, gathered)


def side_halo(parts, tiles_ref, masks_ref, halo_ref):
    others, size = tiles_ref.shape[2:4]
    halos = [jnp.zeros((ROWS, size), jnp.float32) for _ in range(REACH)]
    for i in range(REACH):
        entries = times_tiles(parts, slice(i * size, (i + 1) * size), tiles_ref[:, i])
        for s in range(others):
            for t in range(REACH):
                at = (i * others + s) * REACH + t
                halos[t] += jnp.where(masks_ref[at : at + 1, :] > 0, entries[s], 0.0)
    for t in range(REACH):
        halo_ref[:, t * size : (t + 1) * size] = halos[t]


def halos_kernel(*refs):
    field_ref, hbm_refs, halo_refs = refs[0], refs[6:9], refs[9:11]
    staged, scratch, gathered = refs[11:16], refs[16:20], refs[20]

    size = staged[0].shape[3]

    def make_halos(ready):
        parts = [side_parts(which, field_ref, staged[2], size, gathered.at[which]) for which in range(2)]
        for which in range(2):
            ready(which)
            side_halo(parts[which], staged[which], staged[3 + which], halo_refs[which])

    @pl.when(is_late())
    def _():
        for move in moves_of(hbm_refs, staged, scratch):
            move.start()
        stage(hbm_refs, staged, scratch)

        def ready(which):
            for move in moves_of(hbm_refs, staged, scratch, 2 + which, 3 + which):
                move.wait()

        make_halos(ready)

    @pl.when(jnp.logical_not(is_late()))
    def _():
        make_halos(lambda which: None)


def own_kernel(
    field_ref, offsets_hbm, tiles_hbm, galerkin_hbm, rhs_hbm,
    main_ref, offsets, tiles, galerkin, rhs, mixer, mixer_parts, gathered, sems,
):
    _, tile_rows, near, size, _ = tiles.shape
    own = field_ref.shape[1]
    pairs = [(galerkin_hbm, galerkin), (offsets_hbm, offsets), (rhs_hbm, rhs)]
    pairs += [(tiles_hbm.at[:, r], tiles.at[:, r]) for r in range(tile_rows)]
    moves = [pltpu.make_async_copy(a, b, sems.at[i]) for i, (a, b) in enumerate(pairs)]
    for move in moves:
        move.start()
    moves[0].wait()
    set_mixer(mixer_parts, galerkin, mixer, (lax.axis_index("chaos"),))
    parts = mix(field_ref, mixer_parts, 0, slice(None), gathered)
    sums = [jnp.zeros((ROWS, size), jnp.float32) for _ in range(tile_rows)]
    moves[1].wait()
    for r in range(tile_rows):
        moves[3 + r].wait()
        entries = times_tiles(parts, slice(r * size, (r + 1) * size), tiles[:, r])
        sums[r] += entries[0]
        for s in range(1, near):
            for t in range(tile_rows):
                if abs(t - r) > REACH or t == r:
                    continue
                sums[t] += jnp.where(r + offsets[r, s] == t, entries[s], 0.0)
    moves[2].wait()
    for t in range(tile_rows):
        columns = slice(t * size, (t + 1) * size)
        main_ref[:, columns] = rhs[:, columns] - sums[t][:own]


def body(adjoint_field, stiffness_tiles, offsets, galerkin, adjoint_rhs):
    terms, tile_rows, near, size, _ = stiffness_tiles.shape
    own, dofs = adjoint_field.shape
    groups, slabs = lax.axis_size("chaos"), lax.axis_size("space")
    chaos = own * groups
    vmem = pl.BlockSpec(memory_space=pltpu.VMEM)
    hbm = pl.BlockSpec(memory_space=pltpu.HBM)
    params = pltpu.CompilerParams(vmem_limit_bytes=24 * 1024 * 1024)
    all_tiles, rhs = in_hbm(stiffness_tiles), in_hbm(adjoint_rhs)

    def floats(*shape):
        return jax.ShapeDtypeStruct(shape, jnp.float32)

    def halves(*shape):
        return jax.ShapeDtypeStruct(shape, jnp.bfloat16)

    side = (terms, REACH, near - 1, size, size)
    side_masks = REACH * (near - 1) * REACH
    staged_shapes = (
        pltpu.VMEM(side, jnp.bfloat16),
        pltpu.VMEM(side, jnp.bfloat16),
        pltpu.VMEM((SIDES, 2 * terms * ROWS, chaos), jnp.bfloat16),
        pltpu.VMEM((side_masks, size), jnp.float32),
        pltpu.VMEM((side_masks, size), jnp.float32),
    )
    stage_scratch = [
        pltpu.SMEM(offsets.shape, jnp.int32),
        pltpu.VMEM((terms, chaos, chaos), jnp.float32),
        pltpu.VMEM((SIDES, terms, ROWS, chaos), jnp.float32),
        pltpu.SemaphoreType.DMA((4,)),
    ]
    sources = in_hbm(offsets), all_tiles, in_hbm(galerkin)
    copies, *staged = pl.pallas_call(
        stage_kernel,
        out_shape=(halves(groups, own, dofs), *staged_shapes),
        in_specs=[hbm] * 4,
        out_specs=(vmem,) * 6,
        scratch_shapes=[*stage_scratch, pltpu.VMEM((own, dofs), jnp.bfloat16), pltpu.SemaphoreType.DMA],
        compiler_params=params,
    )(in_hbm(adjoint_field), *sources)

    field = lax.all_to_all(copies, "chaos", 0, 0)

    halo = floats(ROWS, REACH * size)
    first, second, *_ = pl.pallas_call(
        halos_kernel,
        out_shape=(halo, halo, *staged_shapes),
        in_specs=[vmem] * 6 + [hbm] * 3,
        out_specs=(vmem,) * 7,
        input_output_aliases={1 + i: 2 + i for i in range(5)},
        scratch_shapes=[*stage_scratch, pltpu.VMEM((SIDES, chaos, REACH * size), jnp.float32)],
        compiler_params=params,
    )(field, *map(in_vmem, staged), *sources)
    main = pl.pallas_call(
        own_kernel,
        out_shape=floats(own, dofs),
        in_specs=[vmem] + [hbm] * 4,
        out_specs=vmem,
        scratch_shapes=[
            pltpu.SMEM(offsets.shape, jnp.int32),
            pltpu.VMEM(stiffness_tiles.shape, jnp.bfloat16),
            pltpu.VMEM((terms, chaos, chaos), jnp.float32),
            pltpu.VMEM((own, dofs), jnp.float32),
            pltpu.VMEM((1, terms, ROWS, chaos), jnp.float32),
            pltpu.VMEM((1, 2 * terms * ROWS, chaos), jnp.bfloat16),
            pltpu.VMEM((chaos, dofs), jnp.float32),
            pltpu.SemaphoreType.DMA((3 + tile_rows,)),
        ],
        compiler_params=params,
    )(field, *sources, rhs)

    def partner(s, c):
        return (s + 1) * groups + (across(c) if s % RUN == RUN - 1 else c)

    pairs = [(s * groups + c, partner(s, c), s) for s in range(slabs - 1) for c in range(groups)]
    axes = ("space", "chaos")

    def swap(x, parity):
        return lax.ppermute(x, axes, [p for a, b, s in pairs if s % 2 == parity for p in ((a, b), (b, a))])

    got_first, got_second = swap(first, 1), swap(second, 0)
    even = (lax.axis_index("space") % 2) == 0
    halo_a = jnp.where(even, got_first, got_second)
    halo_b = jnp.where(even, got_second, got_first)
    got = jnp.concatenate([halo_a, halo_b], axis=1)
    return main - got[:own]


def solution(mesh):
    return jax.shard_map(
        body,
        mesh=mesh,
        in_specs=(
            P("chaos", "space"),
            P(None, "space", None, None, None),
            P("space", None),
            P(),
            P("chaos", "space"),
        ),
        out_specs=P("chaos", "space"),
        check_vma=False,
    )
```

```python
import jax
import jax.numpy as jnp
from jax import lax
from jax.experimental import pallas as pl
from jax.experimental.pallas import tpu as pltpu
from jax.sharding import PartitionSpec as P

ROWS = 8
REACH = 2
SPAN = 2 * REACH + 1
RUN = 4
ACROSS = (3, 2, 1, 0)
SIDES = 2


def across(c):
    return 2 * ACROSS[c // 2] + 1 - c % 2


def is_late():
    upper = lax.rem(lax.axis_index("space") // RUN, 2)
    return lax.axis_index("chaos") // 2 == (1 - upper) * (lax.axis_size("chaos") // 2 - 1)


def in_vmem(x):
    return pltpu.with_memory_space_constraint(x, pltpu.VMEM)


def in_hbm(x):
    return pltpu.with_memory_space_constraint(x, pltpu.HBM)


def split(x):
    high = x.astype(jnp.bfloat16).astype(jnp.float32)
    return high, x - high


def moves_of(hbm_refs, staged, scratch, first=0, last=4):
    offsets_hbm, tiles_hbm, galerkin_hbm = hbm_refs
    offsets, galerkin, _, sems = scratch
    tile_rows, near = tiles_hbm.shape[1:3]
    first_row, second_row = side_rows(tile_rows)
    pairs = [(galerkin_hbm, galerkin), (offsets_hbm, offsets)]
    for row, out in zip((first_row, second_row), staged[:2]):
        pairs.append((tiles_hbm.at[:, pl.ds(row, REACH), 1:near], out))
    return [pltpu.make_async_copy(*pairs[i], sems.at[i]) for i in range(first, last)]


def side_rows(tile_rows):
    odd = lax.rem(lax.axis_index("space"), 2)
    return odd * (tile_rows - REACH), (1 - odd) * (tile_rows - REACH)


def set_mixer(mixer_out, galerkin, mixer, owners):
    terms = galerkin.shape[0]
    own = galerkin.shape[1] // lax.axis_size("chaos")
    mixer[...] = jnp.zeros_like(mixer)
    for b, owner in enumerate(owners):
        for k in range(terms):
            mixer[b, k, :own, :] = galerkin[k, pl.ds(owner * own, own), :]
    parts = split(mixer[...].reshape(len(owners), terms * ROWS, galerkin.shape[1]))
    mixer_out[...] = jnp.concatenate(parts, axis=1).astype(jnp.bfloat16)


def stage(hbm_refs, staged, scratch):
    _, _, mixer_out, first_masks, second_masks = staged
    offsets, galerkin, mixer, _ = scratch
    moves = moves_of(hbm_refs, staged, scratch, 0, 2)
    tile_rows, near = hbm_refs[1].shape[1:3]
    groups = lax.axis_size("chaos")
    space, block = lax.axis_index("space"), lax.axis_index("chaos")
    moves[0].wait()
    place = lax.rem(space, RUN)
    at_end = jnp.logical_or(place == 0, place == RUN - 1)
    far_off = block
    for c in range(groups):
        here = jnp.where(place == 0, across(c) == block, c == block)
        far_off = jnp.where(here, jnp.where(place == 0, c, across(c)), far_off)
    set_mixer(mixer_out, galerkin, mixer, (jnp.where(at_end, far_off, block), block))
    moves[1].wait()

    first_row, second_row = side_rows(tile_rows)

    def row_of(flag):
        return jnp.full((1, first_masks.shape[1]), flag.astype(jnp.float32))

    for row, out in ((first_row, first_masks), (second_row, second_masks)):
        below = jnp.where(row == 0, -REACH, tile_rows)
        for i in range(REACH):
            for s in range(1, near):
                for t in range(REACH):
                    at = (i * (near - 1) + s - 1) * REACH + t
                    out[at : at + 1, :] = row_of(row + i + offsets[row + i, s] == below + t)


def stage_kernel(
    field_ref, offsets_hbm, tiles_hbm, galerkin_hbm,
    copies_out, first_tiles, second_tiles, mixer_out, first_masks, second_masks,
    offsets, galerkin, mixer, sems, field, field_sem,
):
    hbm_refs = offsets_hbm, tiles_hbm, galerkin_hbm
    staged = first_tiles, second_tiles, mixer_out, first_masks, second_masks
    scratch = offsets, galerkin, mixer, sems
    get_field = pltpu.make_async_copy(field_ref, field, field_sem)
    get_field.start()

    @pl.when(jnp.logical_not(is_late()))
    def _():
        for move in moves_of(hbm_refs, staged, scratch):
            move.start()

    get_field.wait()
    value = field[...]
    for g in range(copies_out.shape[0]):
        copies_out[g] = value

    @pl.when(jnp.logical_not(is_late()))
    def _():
        stage(hbm_refs, staged, scratch)
        for move in moves_of(hbm_refs, staged, scratch, 2):
            move.wait()


def mix(field_ref, mixer_ref, block, columns, gathered):
    groups, own, _ = field_ref.shape
    rows = mixer_ref.shape[1] // 2
    for g in range(groups):
        gathered[g * own : (g + 1) * own, :] = field_ref[g, :, columns].astype(jnp.float32)
    field = gathered[...].astype(jnp.bfloat16)
    both = jnp.dot(mixer_ref[block], field, preferred_element_type=jnp.float32)
    mixed = (both[:rows] + both[rows:]).reshape(rows // ROWS, ROWS, field.shape[1])
    return split(mixed)


def times_tiles(parts, columns, tiles):
    terms, near, size, _ = tiles.shape
    left = jnp.concatenate(
        [jnp.concatenate([part[k, :, columns] for part in parts], axis=0) for k in range(terms)],
        axis=1,
    ).astype(jnp.bfloat16)
    right = jnp.concatenate([tiles[:, s].reshape(terms * size, size) for s in range(near)], axis=1)
    product = jnp.dot(left, right, preferred_element_type=jnp.float32)
    product = product[:ROWS] + product[ROWS:]
    return [product[:, s * size : (s + 1) * size] for s in range(near)]


def side_parts(which, field_ref, mixer_ref, size, gathered):
    row = side_rows(field_ref.shape[2] // size)[which]
    columns = pl.ds(pl.multiple_of(row * size, size), REACH * size)
    return mix(field_ref, mixer_ref, which, columns, gathered)


def side_halo(parts, tiles_ref, masks_ref, halo_ref):
    others, size = tiles_ref.shape[2:4]
    halos = [jnp.zeros((ROWS, size), jnp.float32) for _ in range(REACH)]
    for i in range(REACH):
        entries = times_tiles(parts, slice(i * size, (i + 1) * size), tiles_ref[:, i])
        for s in range(others):
            for t in range(REACH):
                at = (i * others + s) * REACH + t
                halos[t] += jnp.where(masks_ref[at : at + 1, :] > 0, entries[s], 0.0)
    for t in range(REACH):
        halo_ref[:, t * size : (t + 1) * size] = halos[t]


def halos_kernel(*refs):
    field_ref, hbm_refs, halo_refs = refs[0], refs[6:9], refs[9:11]
    staged, scratch, gathered = refs[11:16], refs[16:20], refs[20]

    size = staged[0].shape[3]

    def make_halos(ready):
        parts = [side_parts(which, field_ref, staged[2], size, gathered.at[which]) for which in range(2)]
        for which in range(2):
            ready(which)
            side_halo(parts[which], staged[which], staged[3 + which], halo_refs[which])

    @pl.when(is_late())
    def _():
        for move in moves_of(hbm_refs, staged, scratch):
            move.start()
        stage(hbm_refs, staged, scratch)

        def ready(which):
            for move in moves_of(hbm_refs, staged, scratch, 2 + which, 3 + which):
                move.wait()

        make_halos(ready)

    @pl.when(jnp.logical_not(is_late()))
    def _():
        make_halos(lambda which: None)


def own_kernel(
    field_ref, offsets_hbm, tiles_hbm, galerkin_hbm, rhs_hbm,
    main_ref, offsets, tiles, galerkin, rhs, mixer, mixer_parts, gathered, sems,
):
    _, tile_rows, near, size, _ = tiles.shape
    own = field_ref.shape[1]
    pairs = [(galerkin_hbm, galerkin), (offsets_hbm, offsets), (rhs_hbm, rhs)]
    pairs += [(tiles_hbm.at[:, r], tiles.at[:, r]) for r in range(tile_rows)]
    moves = [pltpu.make_async_copy(a, b, sems.at[i]) for i, (a, b) in enumerate(pairs)]
    for move in moves:
        move.start()
    moves[0].wait()
    set_mixer(mixer_parts, galerkin, mixer, (lax.axis_index("chaos"),))
    parts = mix(field_ref, mixer_parts, 0, slice(None), gathered)
    sums = [jnp.zeros((ROWS, size), jnp.float32) for _ in range(tile_rows)]
    moves[1].wait()
    for r in range(tile_rows):
        moves[3 + r].wait()
        entries = times_tiles(parts, slice(r * size, (r + 1) * size), tiles[:, r])
        sums[r] += entries[0]
        for s in range(1, near):
            for t in range(tile_rows):
                if abs(t - r) > REACH or t == r:
                    continue
                sums[t] += jnp.where(r + offsets[r, s] == t, entries[s], 0.0)
    moves[2].wait()
    for t in range(tile_rows):
        columns = slice(t * size, (t + 1) * size)
        main_ref[:, columns] = rhs[:, columns] - sums[t][:own]


def body(adjoint_field, stiffness_tiles, offsets, galerkin, adjoint_rhs):
    terms, tile_rows, near, size, _ = stiffness_tiles.shape
    own, dofs = adjoint_field.shape
    groups, slabs = lax.axis_size("chaos"), lax.axis_size("space")
    chaos = own * groups
    vmem = pl.BlockSpec(memory_space=pltpu.VMEM)
    hbm = pl.BlockSpec(memory_space=pltpu.HBM)
    params = pltpu.CompilerParams(vmem_limit_bytes=24 * 1024 * 1024)
    all_tiles, rhs = in_hbm(stiffness_tiles), in_hbm(adjoint_rhs)

    def floats(*shape):
        return jax.ShapeDtypeStruct(shape, jnp.float32)

    def halves(*shape):
        return jax.ShapeDtypeStruct(shape, jnp.bfloat16)

    side = (terms, REACH, near - 1, size, size)
    side_masks = REACH * (near - 1) * REACH
    staged_shapes = (
        pltpu.VMEM(side, jnp.bfloat16),
        pltpu.VMEM(side, jnp.bfloat16),
        pltpu.VMEM((SIDES, 2 * terms * ROWS, chaos), jnp.bfloat16),
        pltpu.VMEM((side_masks, size), jnp.float32),
        pltpu.VMEM((side_masks, size), jnp.float32),
    )
    stage_scratch = [
        pltpu.SMEM(offsets.shape, jnp.int32),
        pltpu.VMEM((terms, chaos, chaos), jnp.float32),
        pltpu.VMEM((SIDES, terms, ROWS, chaos), jnp.float32),
        pltpu.SemaphoreType.DMA((4,)),
    ]
    sources = in_hbm(offsets), all_tiles, in_hbm(galerkin)
    copies, *staged = pl.pallas_call(
        stage_kernel,
        out_shape=(halves(groups, own, dofs), *staged_shapes),
        in_specs=[hbm] * 4,
        out_specs=(vmem,) * 6,
        scratch_shapes=[*stage_scratch, pltpu.VMEM((own, dofs), jnp.bfloat16), pltpu.SemaphoreType.DMA],
        compiler_params=params,
    )(in_hbm(adjoint_field), *sources)

    field = lax.all_to_all(copies, "chaos", 0, 0)

    halo = floats(ROWS, REACH * size)
    first, second, *_ = pl.pallas_call(
        halos_kernel,
        out_shape=(halo, halo, *staged_shapes),
        in_specs=[vmem] * 6 + [hbm] * 3,
        out_specs=(vmem,) * 7,
        input_output_aliases={1 + i: 2 + i for i in range(5)},
        scratch_shapes=[*stage_scratch, pltpu.VMEM((SIDES, chaos, REACH * size), jnp.float32)],
        compiler_params=params,
    )(field, *map(in_vmem, staged), *sources)
    main = pl.pallas_call(
        own_kernel,
        out_shape=floats(own, dofs),
        in_specs=[vmem] + [hbm] * 4,
        out_specs=vmem,
        scratch_shapes=[
            pltpu.SMEM(offsets.shape, jnp.int32),
            pltpu.VMEM(stiffness_tiles.shape, jnp.bfloat16),
            pltpu.VMEM((terms, chaos, chaos), jnp.float32),
            pltpu.VMEM((own, dofs), jnp.float32),
            pltpu.VMEM((1, terms, ROWS, chaos), jnp.float32),
            pltpu.VMEM((1, 2 * terms * ROWS, chaos), jnp.bfloat16),
            pltpu.VMEM((chaos, dofs), jnp.float32),
            pltpu.SemaphoreType.DMA((3 + tile_rows,)),
        ],
        compiler_params=params,
    )(field, *sources, rhs)

    def partner(s, c):
        return (s + 1) * groups + (across(c) if s % RUN == RUN - 1 else c)

    pairs = [(s * groups + c, partner(s, c), s) for s in range(slabs - 1) for c in range(groups)]
    axes = ("space", "chaos")

    def swap(x, parity):
        return lax.ppermute(x, axes, [p for a, b, s in pairs if s % 2 == parity for p in ((a, b), (b, a))])

    got_first, got_second = swap(first, 1), swap(second, 0)
    even = (lax.axis_index("space") % 2) == 0
    halo_a = jnp.where(even, got_first, got_second)
    halo_b = jnp.where(even, got_second, got_first)
    got = jnp.concatenate([halo_a, halo_b], axis=1)
    return main - got[:own]


def solution(mesh):
    return jax.shard_map(
        body,
        mesh=mesh,
        in_specs=(
            P("chaos", "space"),
            P(None, "space", None, None, None),
            P("space", None),
            P(),
            P("chaos", "space"),
        ),
        out_specs=P("chaos", "space"),
        check_vma=False,
    )
```
